512 devices in a mesh: group: 8 (over x, core), shard: 16 (over z_hi, y), col: 4 (over z_lo).
Axes of the slice: x: 4, y: 4, z: 16 (z_hi: 4, z_lo: 4; z = z_hi * 4 + z_lo), core: 2. Of those that a mesh axis runs over, the one named last changes fastest.
Arguments:
- master: bfloat16 [4, 1024, 5120], P('col', 'group', 'shard'), may hold values from -0.09375 to 0.09375
- grad: bfloat16 [4, 1024, 5120], P('col', 'group', 'shard'), may hold values from -6 to 6
- first: bfloat16 [4, 1024, 5120], P('col', 'group', 'shard'), may hold values from -0.59765625 to 0.59765625
- second: bfloat16 [4, 1024, 5120], P('col', 'group', 'shard'), may hold values from 0.0009994507 to 1
- resident: bfloat16 [8, 4096, 5120], P('group', 'col', 'shard'), may hold values from -0.09375 to 0.09375
- tags: int32 [8], P('group'), may hold values from 0 to 15, as said below
- queries: bfloat16 [8, 4, 4096], P('group', None, 'col'), may hold values from -70 to 70
- key_cache: bfloat16 [8, 4, 8192, 1024], P('group', None, 'shard', 'col'), may hold values from -8 to 8
- value_cache: bfloat16 [8, 4, 8192, 1024], P('group', None, 'shard', 'col'), may hold values from -6 to 6
- lengths: int32 [8, 4], P('group'), may hold values from 1024 to 8192, as said below
Outputs:
- new_master: bfloat16 [4, 1024, 5120], P('col', 'group', 'shard')
- new_first: bfloat16 [4, 1024, 5120], P('col', 'group', 'shard')
- new_second: bfloat16 [4, 1024, 5120], P('col', 'group', 'shard')
- projected: bfloat16 [8, 4, 5120], P('group', None, 'shard')
The draws below stay inside these ranges and needn't reach their ends.
Inputs may be any that keep to these rules, and one draw needn't show every extreme that they name: `tags`: at least one replica has an odd version and at least one an even version; some replica has version 15. `lengths`: some row has exactly 8192.
All inputs are finite; a program needn't handle non-finite values.
Results may differ from the reference program's by a relative error of at most 0.012.
Values may be sent and summed in bfloat16 or wider, within the bound.
A program may use at most 64 MiB of HBM per device.

```python
import math
import jax
import jax.numpy as jnp
from jax import lax

D = 5120
KVH = 8
HS = 128
ROWS = 4
HD = 4096
GQ = 4
CTX = 8192
N_GROUP = 8
N_COL = 4


def draw_queries(key, part):
    key = jax.random.fold_in(key, 1)
    base = 3.0 * jax.random.normal(key, (N_GROUP, ROWS, HD))
    return jnp.clip(base, -18.0, 18.0).astype(jnp.bfloat16)


def draw_key_cache(key, part):
    key = jax.random.fold_in(key, 2)
    base = jax.random.normal(key, (N_GROUP, ROWS, CTX, KVH * HS))
    return jnp.clip(base, -6.0, 6.0).astype(jnp.bfloat16)


def draw_tags(key, part):
    key = jax.random.fold_in(key, 3)
    order_key, high_key = jax.random.split(key)
    order = jax.random.permutation(order_key, N_GROUP)
    high = jax.random.randint(high_key, (N_GROUP,), 0, 8)
    high = jnp.where(order == 1, 7, high)
    return (2 * high + order % 2).astype(jnp.int32)


def draw_lengths(key, part):
    key = jax.random.fold_in(key, 4)
    first_key, second_key = jax.random.split(key)
    base = jax.random.randint(first_key, (N_GROUP * ROWS,), CTX // 8, CTX + 1)
    chosen = jax.random.randint(second_key, (), 0, N_GROUP * ROWS)
    base = jnp.where(jnp.arange(N_GROUP * ROWS) == chosen, CTX, base)
    return base.reshape(N_GROUP, ROWS).astype(jnp.int32)


def block_scale(own_key, extent, cuts, low, high):
    def one(dim, blocks):
        heights = jax.random.uniform(jax.random.fold_in(jax.random.fold_in(own_key, 6), dim), (blocks,), jnp.float32, low / len(cuts), high / len(cuts))
        return jnp.repeat(jnp.exp(heights), extent[dim] // blocks).reshape((-1,) + (1,) * (len(extent) - dim - 1))

    factor_of = one(*cuts[0])
    for cut in cuts[1:]:
        factor_of = factor_of * one(*cut)
    return factor_of


def gaussian(own_key, shape, spread, most, cuts=(), kind=jnp.bfloat16):
    gain = block_scale(own_key, shape, cuts, -0.22, 0.18) if cuts else 1.0
    entries = jax.random.normal(own_key, shape, jnp.float32) * spread * gain
    return jnp.minimum(jnp.maximum(entries, -most), most).astype(kind)


def setup_inputs(seed: int = 0) -> dict:
    splits = jax.random.split(jax.random.key(seed), 11)
    return {
        "master": gaussian(splits[0], (N_COL, HD // N_COL, D), HD ** -0.5, 0.09375, ((0, 4), (1, 8), (2, 16))),
        "grad": gaussian(splits[1], (N_COL, HD // N_COL, D), 1.0, 6.0, ((0, 4), (1, 8), (2, 16))),
        "first": gaussian(splits[2], (N_COL, HD // N_COL, D), 0.1, 0.59765625, ((0, 4), (1, 8), (2, 16))),
        "second": jnp.clip(jnp.exp(math.log(1.0) - 6.9083047 * jax.random.uniform(splits[3], (N_COL, HD // N_COL, D), jnp.float32) ** block_scale(splits[3], (N_COL, HD // N_COL, D), ((0, 4), (1, 8), (2, 16)), -0.2, 0.2)), 0.0009994507, 1.0).astype(jnp.bfloat16),
        "resident": gaussian(splits[4], (N_GROUP, HD, D), HD ** -0.5, 0.09375, ((0, 8), (1, 4), (2, 16))),
        "tags": draw_tags(jax.random.fold_in(splits[10], 71), 0),
        "queries": draw_queries(jax.random.fold_in(splits[10], 71), 0),
        "key_cache": draw_key_cache(jax.random.fold_in(splits[10], 71), 0),
        "value_cache": gaussian(splits[8], (N_GROUP, ROWS, CTX, KVH * HS), 1.0, 6.0, ((0, 8), (2, 16), (3, 4))),
        "lengths": draw_lengths(jax.random.fold_in(splits[10], 71), 0),
    }


beta_one = 0.9
beta_two = 0.999
learn_rate = 0.01
decay = 0.1
adam_eps = 1e-08
correct_one = 1.0
correct_two = 0.6323045752
neg_big = -1e+30

def reference(master, grad, first, second, resident, tags, queries, key_cache, value_cache, lengths):
    g32 = grad.astype(jnp.float32)
    first_new = beta_one * first.astype(jnp.float32) + (1.0 - beta_one) * g32
    second_new = beta_two * second.astype(jnp.float32) + (1.0 - beta_two) * g32 * g32
    w32 = master.astype(jnp.float32)
    step_size = learn_rate * (first_new / correct_one) / (jnp.sqrt(second_new / correct_two) + adam_eps)
    updated = (w32 - step_size - learn_rate * decay * w32).astype(jnp.bfloat16)
    w_full = updated.reshape(HD, D)
    scale = 1.0 / HS ** 0.5

    def one_group(items):
        query, keys, values, length, held, version = items
        q32 = query.astype(jnp.float32).reshape(ROWS, KVH, GQ, HS)
        k32 = keys.astype(jnp.float32).reshape(ROWS, CTX, KVH, HS)
        v32 = values.astype(jnp.float32).reshape(ROWS, CTX, KVH, HS)
        scores = jnp.einsum('rkgd,rpkd->rkgp', q32, k32) * scale
        valid = jnp.arange(CTX, dtype=jnp.int32)[None, :] < length[:, None]
        mask = valid[:, None, None, :]
        best = lax.optimization_barrier(jnp.max(jnp.where(mask, scores, neg_big), axis=-1))
        probs = jnp.where(mask, jnp.exp(scores - best[..., None]), 0.0)
        total = lax.optimization_barrier(jnp.sum(probs, axis=-1))
        rounded = probs.astype(jnp.bfloat16).astype(jnp.float32)
        accum = jnp.einsum('rkgp,rpkd->rkgd', rounded, v32)
        attended = (accum / total[..., None]).astype(jnp.bfloat16).reshape(ROWS, HD)
        weights = jnp.where(version % 2 == 1, w_full, held)
        return jnp.dot(attended, weights, preferred_element_type=jnp.float32).astype(jnp.bfloat16)
    projected = lax.map(one_group, (queries, key_cache, value_cache, lengths, resident, tags))
    return (updated, first_new.astype(jnp.bfloat16), second_new.astype(jnp.bfloat16), projected)
```

```python
import functools

import jax
import jax.numpy as jnp
from jax import lax
from jax.experimental import pallas as pl
from jax.experimental.pallas import tpu as pltpu
from jax.sharding import PartitionSpec as P

HS = 128
MESH = pl.DeviceIdType.MESH
F32 = jnp.float32
BF16 = jnp.bfloat16

beta_one = 0.9
beta_two = 0.999
learn_rate = 0.01
decay = 0.1
adam_eps = 1e-08
correct_one = 1.0
correct_two = 0.6323045752
neg_big = -1e30


def adam(master, grad, first, second):
    g32 = grad.astype(F32)
    first_new = beta_one * first.astype(F32) + (1.0 - beta_one) * g32
    second_new = beta_two * second.astype(F32) + (1.0 - beta_two) * g32 * g32
    w32 = master.astype(F32)
    step_size = (
        learn_rate * (first_new / correct_one) / (jnp.sqrt(second_new / correct_two) + adam_eps)
    )
    updated = w32 - step_size - learn_rate * decay * w32
    return updated.astype(BF16), first_new.astype(BF16), second_new.astype(BF16)


def nt(a, b):
    return lax.dot_general(a, b, (((1,), (1,)), ((), ())), preferred_element_type=F32)


def pack(acc, best, total):
    lane = lax.broadcasted_iota(jnp.int32, acc.shape, 1)
    high = total.astype(BF16).astype(F32)
    stats = jnp.where(lane == 0, best, jnp.where(lane == 1, high, jnp.where(lane == 2, total - high, 0.0)))
    return acc, stats


def merge(shares):
    parts = [shares[i].astype(F32) for i in range(4)]
    bests = [part[8:, 0:1] for part in parts]
    best = jnp.maximum(jnp.maximum(bests[0], bests[1]), jnp.maximum(bests[2], bests[3]))
    acc, total = 0.0, 0.0
    for part, own in zip(parts, bests):
        factor = jnp.exp(own - best)
        acc = acc + part[:8] * factor
        total = total + (part[8:, 1:2] + part[8:, 2:3]) * factor
    return acc, best, total


def kernel(
    master_ref, grad_ref, first_ref, second_ref, resident_ref, tags_ref, queries_ref, keys_ref, values_ref, lengths_ref,
    out_ref,
    master, grad, first, second, resident, tags, queries, keys, values, lengths,
    slabs, chosen, y_out, y_in, z_out, z_in, a_in, c_in,
    load_sem, key_sem, value_sem,
    wx_send, wx_recv, ws_send, ws_recv,
    y_send, y_recv, z_send, z_recv, a_send, a_recv, c_send, c_recv,
):
    group = lax.axis_index("group")
    shard = lax.axis_index("shard")
    col = lax.axis_index("col")
    x, core = group // 2, group % 2
    z, y = shard // 4, shard % 4

    def x_peer(d):
        return {"group": (x + d) % 4 * 2 + core}

    def y_peer(d):
        return {"shard": z * 4 + (y + d) % 4}

    def z_peer(d):
        return {"shard": (z + d) % 4 * 4 + y}

    def c_peer(d):
        return {"col": (col + d) % 4}

    sibling = {"group": x * 2 + 1 - core}

    def load(i, src, dst):
        copy = pltpu.make_async_copy(src, dst, load_sem.at[i])
        copy.start()
        return copy

    q_load = load(0, queries_ref, queries)
    l_load = load(1, lengths_ref, lengths)
    k_loads = [pltpu.make_async_copy(keys_ref.at[0, r], keys.at[r], key_sem.at[r]) for r in range(4)]
    v_loads = [pltpu.make_async_copy(values_ref.at[0, r], values.at[r], value_sem.at[r]) for r in range(4)]
    w_loads = [
        load(2 + i, src, dst)
        for i, (src, dst) in enumerate(
            ((master_ref, master), (grad_ref, grad), (first_ref, first), (second_ref, second))
        )
    ]
    for copy in k_loads + v_loads:
        copy.start()
    r_load = load(6, resident_ref, resident)
    t_load = load(7, tags_ref, tags)

    barrier = pltpu.get_barrier_semaphore()
    for d in (1, 2, 3):
        for peer in (x_peer(d), y_peer(d), z_peer(d), c_peer(d)):
            pl.semaphore_signal(barrier, inc=1, device_id=peer, device_id_type=MESH)
    pl.semaphore_signal(barrier, inc=1, device_id=sibling, device_id_type=MESH)

    for copy in w_loads:
        copy.wait()
    slabs[group] = adam(master[0], grad[0], first[0], second[0])[0]
    pl.semaphore_wait(barrier, 13)

    def send(src, dst, send_sem, recv_sem, peer):
        copy = pltpu.make_async_remote_copy(
            src_ref=src, dst_ref=dst, send_sem=send_sem, recv_sem=recv_sem, device_id=peer, device_id_type=MESH
        )
        copy.start()
        return copy

    own_w = [send(slabs.at[group], slabs.at[group], ws_send.at[0], ws_recv.at[0], sibling)]
    for d in (1, 3, 2):
        own_w.append(send(slabs.at[group], slabs.at[group], wx_send.at[d - 1], wx_recv.at[d - 1], x_peer(d)))

    q_load.wait()
    l_load.wait()
    q32 = queries[0].astype(F32)
    tall = [jnp.concatenate([q32[:, h * HS : (h + 1) * HS] for h in range(4 * k, 4 * k + 4)], axis=0) for k in (0, 1)]
    blank = jnp.zeros((16, HS), F32)
    wide = jnp.concatenate(
        [jnp.concatenate([tall[0], blank], axis=1), jnp.concatenate([blank, tall[1]], axis=1)], axis=0
    )
    row_q = lax.broadcasted_iota(jnp.int32, (32, 2 * HS), 0) % 4
    scores = jnp.zeros((32, 512), F32)
    for r in range(4):
        k_loads[r].wait()
        scores = scores + nt(jnp.where(row_q == r, wide, 0.0).astype(BF16), keys[r])
    scores = scores * (1.0 / HS**0.5)
    row = lax.broadcasted_iota(jnp.int32, (32, 512), 0) % 4
    position = shard * 512 + lax.broadcasted_iota(jnp.int32, (32, 512), 1)
    limit = jnp.where(
        row == 0, lengths[0, 0], jnp.where(row == 1, lengths[0, 1], jnp.where(row == 2, lengths[0, 2], lengths[0, 3]))
    )
    mask = position < limit
    best = jnp.max(jnp.where(mask, scores, neg_big), axis=1, keepdims=True)
    best = best.astype(BF16).astype(F32)
    probs = jnp.where(mask, jnp.exp(scores - best), 0.0)
    total = jnp.sum(probs, axis=1, keepdims=True)
    both = jnp.zeros((32, 2 * HS), F32)
    for r in range(4):
        v_loads[r].wait()
        both = both + jnp.dot(
            jnp.where(row == r, probs, 0.0).astype(BF16), values[r], preferred_element_type=F32
        )
    acc = jnp.concatenate([both[:16, :HS], both[16:, HS:]], axis=0)

    acc, stats = pack(acc, best, total)
    for j in range(4):
        y_out[j] = jnp.concatenate([acc[8 * j : 8 * j + 8], stats[8 * j : 8 * j + 8]], axis=0).astype(BF16)
    sent = []
    for d in (2, 1, 3):
        sent.append(send(y_out.at[(y + d) % 4], y_in.at[y], y_send.at[d - 1], y_recv.at[d - 1], y_peer(d)))
    y_in[y] = y_out[y]
    for copy in sent:
        copy.wait_recv()
    acc, best, total = merge(y_in)
    acc, stats = pack(acc, best, total)
    z_out[...] = jnp.concatenate([acc, stats], axis=0).astype(BF16)
    for d in (2, 1, 3):
        sent.append(send(z_out, z_in.at[z], z_send.at[d - 1], z_recv.at[d - 1], z_peer(d)))
    z_in[z] = z_out[...]

    passed = []
    for d in (1, 3, 2):
        own_w[(1, 3, 2).index(d) + 1].wait_recv()
        block = (x + 4 - d) % 4 * 2 + core
        passed.append(send(slabs.at[block], slabs.at[block], ws_send.at[d], ws_recv.at[d], sibling))
    r_load.wait()
    t_load.wait()
    odd = jnp.full((320, HS), tags[0], jnp.int32) % 2 == 1
    own_w[0].wait_recv()
    for copy in passed:
        copy.wait_recv()
    for h in range(8):
        place = (h % 2 * 4 + h // 2) * HS
        chosen[:, place : place + HS] = jnp.where(odd, slabs[h], resident[0, :, h * HS : (h + 1) * HS])

    for copy in sent[3:]:
        copy.wait_recv()
    acc, _, total = merge(z_in)
    a_in[y] = acc / total
    for d in (2, 1, 3):
        sent.append(send(a_in.at[y], a_in.at[y], a_send.at[d - 1], a_recv.at[d - 1], y_peer(d)))
    for copy in sent[6:]:
        copy.wait_recv()
    attended = jnp.concatenate([a_in[j] for j in range(4)], axis=1).astype(BF16)
    even = nt(attended, chosen[:, : 4 * HS])
    uneven = nt(attended, chosen[:, 4 * HS :])
    share = even[:4] + uneven[4:]
    c_in[col] = jnp.concatenate(
        [
            share[:, :HS],
            share[:, HS : 2 * HS],
            jnp.concatenate([share[:, 2 * HS :], jnp.zeros((4, 64), F32)], axis=1),
            jnp.zeros((4, HS), F32),
        ],
        axis=0,
    ).astype(BF16)
    for d in (3, 2, 1):
        sent.append(send(c_in.at[col], c_in.at[col], c_send.at[d - 1], c_recv.at[d - 1], c_peer(d)))
    for copy in sent[9:]:
        copy.wait_recv()
    final = c_in[0].astype(F32) + c_in[1].astype(F32) + c_in[2].astype(F32) + c_in[3].astype(F32)
    out_ref[0] = jnp.concatenate([final[0:4], final[4:8], final[8:12, :64]], axis=1).astype(BF16)
    for copy in own_w + passed + sent:
        copy.wait_send()


def per_device(master, grad, first, second, resident, tags, queries, keys, values, lengths):
    flip = functools.partial(jnp.swapaxes, axis1=1, axis2=2)
    updated, first_new, second_new = adam(master, grad, first, second)
    dma = pltpu.SemaphoreType.DMA
    block = pltpu.VMEM((1, 320, 128), BF16)
    projected = pl.pallas_call(
        kernel,
        out_shape=jax.ShapeDtypeStruct((1, 4, 320), BF16),
        in_specs=[pl.BlockSpec(memory_space=pl.ANY)] * 10,
        out_specs=pl.BlockSpec(memory_space=pltpu.VMEM),
        scratch_shapes=[
            block, block, block, block,
            pltpu.VMEM((1, 320, 1024), BF16),
            pltpu.SMEM((1,), jnp.int32),
            pltpu.VMEM((1, 4, 1024), BF16),
            pltpu.VMEM((4, 512, 256), BF16),
            pltpu.VMEM((4, 512, 256), BF16),
            pltpu.SMEM((1, 4), jnp.int32),
            pltpu.VMEM((8, 320, 128), BF16),
            pltpu.VMEM((320, 1024), BF16),
            pltpu.VMEM((4, 16, 128), BF16),
            pltpu.VMEM((4, 16, 128), BF16),
            pltpu.VMEM((16, 128), BF16),
            pltpu.VMEM((4, 16, 128), BF16),
            pltpu.VMEM((4, 8, 128), F32),
            pltpu.VMEM((4, 16, 128), BF16),
            dma((8,)), dma((4,)), dma((4,)),
            dma((3,)), dma((3,)), dma((4,)), dma((4,)),
            dma((3,)), dma((3,)), dma((3,)), dma((3,)), dma((3,)), dma((3,)), dma((3,)), dma((3,)),
        ],
        compiler_params=pltpu.CompilerParams(collective_id=0, has_side_effects=True),
    )(flip(master), flip(grad), flip(first), flip(second), flip(resident), tags, queries, keys, values, lengths)
    return updated, first_new, second_new, projected


def solution(mesh):
    return jax.shard_map(
        per_device,
        mesh=mesh,
        in_specs=(
            P("col", "group", "shard"),
            P("col", "group", "shard"),
            P("col", "group", "shard"),
            P("col", "group", "shard"),
            P("group", "col", "shard"),
            P("group"),
            P("group", None, "col"),
            P("group", None, "shard", "col"),
            P("group", None, "shard", "col"),
            P("group", None),
        ),
        out_specs=(
            P("col", "group", "shard"),
            P("col", "group", "shard"),
            P("col", "group", "shard"),
            P("group", None, "shard"),
        ),
        check_vma=False,
    )
```

```python
import functools

import jax
import jax.numpy as jnp
from jax import lax
from jax.experimental import pallas as pl
from jax.experimental.pallas import tpu as pltpu
from jax.sharding import PartitionSpec as P

HS = 128
MESH = pl.DeviceIdType.MESH
F32 = jnp.float32
BF16 = jnp.bfloat16

beta_one = 0.9
beta_two = 0.999
learn_rate = 0.01
decay = 0.1
adam_eps = 1e-08
correct_one = 1.0
correct_two = 0.6323045752
neg_big = -1e30


def adam(master, grad, first, second):
    g32 = grad.astype(F32)
    first_new = beta_one * first.astype(F32) + (1.0 - beta_one) * g32
    second_new = beta_two * second.astype(F32) + (1.0 - beta_two) * g32 * g32
    w32 = master.astype(F32)
    step_size = (
        learn_rate * (first_new / correct_one) / (jnp.sqrt(second_new / correct_two) + adam_eps)
    )
    updated = w32 - step_size - learn_rate * decay * w32
    return updated.astype(BF16), first_new.astype(BF16), second_new.astype(BF16)


def nt(a, b):
    return lax.dot_general(a, b, (((1,), (1,)), ((), ())), preferred_element_type=F32)


def pack(acc, best, total):
    lane = lax.broadcasted_iota(jnp.int32, (16, HS), 1)
    high = total.astype(BF16).astype(F32)
    low = total - high
    stats = jnp.zeros((16, HS), F32)
    for i, column in enumerate((best[:16], high[:16], low[:16], best[16:], high[16:], low[16:])):
        stats = jnp.where(lane == i, column, stats)
    return jnp.concatenate([acc, stats], axis=0).astype(BF16)


def merge(shares):
    parts = [shares[i].astype(F32) for i in range(4)]
    bests = [jnp.concatenate([part[32:, 0:1], part[32:, 3:4]], axis=0) for part in parts]
    best = jnp.maximum(jnp.maximum(bests[0], bests[1]), jnp.maximum(bests[2], bests[3]))
    acc, total = 0.0, 0.0
    for part, own in zip(parts, bests):
        factor = jnp.exp(own - best)
        acc = acc + part[:32] * factor
        sums = jnp.concatenate([part[32:, 1:2] + part[32:, 2:3], part[32:, 4:5] + part[32:, 5:6]], axis=0)
        total = total + sums * factor
    return acc, best, total


def kernel(
    master_ref, grad_ref, first_ref, second_ref, resident_ref, tags_ref, queries_ref, keys_ref, values_ref, lengths_ref,
    updated_ref, first_out, second_out, out_ref,
    state, resident, tags, queries, keys, values, lengths,
    slabs, chosen, y_out, y_in, z_out, z_in, c_in,
    z_ready, s_ready, small_sem, key_sem, value_sem, state_sem, resident_sem, tags_sem,
    w_send, x_recv, s_recv, y_send, y_recv, z_send, z_recv, c_send, c_recv,
):
    group = lax.axis_index("group")
    shard = lax.axis_index("shard")
    col = lax.axis_index("col")
    x, core = group // 2, group % 2
    z, y = shard // 4, shard % 4

    x_peers = [{"group": (x + d) % 4 * 2 + core} for d in (1, 2, 3)]
    y_peers = [{"shard": z * 4 + (y + d) % 4} for d in (1, 2, 3)]
    z_peers = [{"shard": (z + d) % 4 * 4 + y} for d in (1, 2, 3)]
    c_peers = [{"col": (col + d) % 4} for d in (1, 2, 3)]
    sibling = {"group": x * 2 + 1 - core}

    def load(src, dst, sem):
        copy = pltpu.make_async_copy(src, dst, sem)
        copy.start()
        return copy

    barrier = pltpu.get_barrier_semaphore()

    def tell(sem, peer):
        pl.semaphore_signal(sem, inc=1, device_id=peer, device_id_type=MESH)

    for peer in y_peers + x_peers + c_peers:
        tell(barrier, peer)
    for j in (1, 2, 3):
        pl.when(z < j)(functools.partial(tell, barrier, {"shard": j * 4 + y}))
    pl.when(core == 0)(functools.partial(tell, barrier, sibling))

    k_loads = [load(keys_ref.at[0, r], keys.at[r], key_sem.at[r]) for r in range(4)]
    q_load = load(queries_ref, queries, small_sem.at[0])
    l_load = load(lengths_ref, lengths, small_sem.at[1])

    v_load = load(values_ref.at[0], values, value_sem)
    for i, src in enumerate((master_ref, grad_ref, first_ref, second_ref)):
        load(src.at[0], state.at[i], state_sem)
    r_load = load(resident_ref, resident, resident_sem)
    t_load = load(tags_ref, tags, tags_sem)

    def send(src, dst, send_sem, recv_sem, peer):
        pltpu.make_async_remote_copy(
            src_ref=src, dst_ref=dst, send_sem=send_sem, recv_sem=recv_sem, device_id=peer, device_id_type=MESH
        ).start()

    def arrive(ref, sem):
        pltpu.make_async_copy(ref, ref, sem).wait()

    q_load.wait()
    l_load.wait()
    q32 = queries[0].astype(F32)
    tall = [jnp.concatenate([q32[:, h * HS : (h + 1) * HS] for h in range(4 * k, 4 * k + 4)], axis=0) for k in (0, 1)]
    blank = jnp.zeros((16, HS), F32)
    wide = jnp.concatenate(
        [jnp.concatenate([tall[0], blank], axis=1), jnp.concatenate([blank, tall[1]], axis=1)], axis=0
    )
    row_q = lax.broadcasted_iota(jnp.int32, (32, 2 * HS), 0) % 4
    row = lax.broadcasted_iota(jnp.int32, (32, 512), 0) % 4
    position = shard * 512 + lax.broadcasted_iota(jnp.int32, (32, 512), 1)
    limit = jnp.where(
        row == 0, lengths[0, 0], jnp.where(row == 1, lengths[0, 1], jnp.where(row == 2, lengths[0, 2], lengths[0, 3]))
    )
    mask = position < limit
    scores = jnp.zeros((32, 512), F32)
    for r in range(4):
        k_loads[r].wait()
        scores = scores + nt(jnp.where(row_q == r, wide, 0.0).astype(BF16), keys[r])
    scores = scores * (1.0 / HS**0.5)
    best = jnp.max(jnp.where(mask, scores, neg_big), axis=1, keepdims=True)
    best = best.astype(BF16).astype(F32)
    probs = jnp.where(mask, jnp.exp(scores - best), 0.0)
    total = jnp.sum(probs, axis=1, keepdims=True)
    v_load.wait()
    both = jnp.zeros((32, 2 * HS), F32)
    for r in range(4):
        both = both + jnp.dot(
            jnp.where(row == r, probs, 0.0).astype(BF16), values[r], preferred_element_type=F32
        )
    y_out[...] = pack(jnp.concatenate([both[:16, :HS], both[16:, HS:]], axis=0), best, total)

    pl.semaphore_wait(barrier, 9 + z + core)
    for j in (0, 1, 2):
        pl.when(j < z)(functools.partial(tell, z_ready, {"shard": j * 4 + y}))
    pl.when(core == 1)(functools.partial(tell, s_ready, sibling))
    for peer in (y_peers[1], y_peers[0], y_peers[2]):
        send(y_out, y_in.at[y], y_send, y_recv, peer)
    y_in[y] = y_out[...]

    arrive(state, state_sem)
    updated, first_new, second_new = adam(state[0], state[1], state[2], state[3])
    slabs[group] = updated
    for d in (1, 3, 2):
        send(slabs.at[group], slabs.at[group], w_send, x_recv.at[d - 1], x_peers[d - 1])
    updated_ref[0] = updated
    first_out[0] = first_new
    second_out[0] = second_new

    arrive(y_in.at[0:3], y_recv)
    z_out[...] = pack(*merge(y_in))
    pl.when(z < 3)(lambda: pl.semaphore_wait(z_ready, 3 - z))
    for peer in (z_peers[1], z_peers[0], z_peers[2]):
        send(z_out, z_in.at[z], z_send, z_recv, peer)
    z_in[z] = z_out[...]

    pl.when(core == 0)(lambda: pl.semaphore_wait(s_ready, 1))
    send(slabs.at[group], slabs.at[group], w_send, s_recv, sibling)
    for d in (1, 3, 2):
        arrive(slabs.at[0], x_recv.at[d - 1])
        block = (x + 4 - d) % 4 * 2 + core
        send(slabs.at[block], slabs.at[block], w_send, s_recv, sibling)
    r_load.wait()
    t_load.wait()
    odd = jnp.full((320, HS), tags[0], jnp.int32) % 2 == 1
    arrive(slabs.at[0:4], s_recv)
    for h in range(8):
        place = (h % 2 * 4 + h // 2) * HS
        chosen[:, place : place + HS] = jnp.where(odd, slabs[h], resident[0, :, h * HS : (h + 1) * HS])

    arrive(z_in.at[0:3], z_recv)
    acc, _, total = merge(z_in)
    acc = acc / total
    attended = jnp.concatenate([acc[8 * j : 8 * j + 8] for j in range(4)], axis=1).astype(BF16)
    even = nt(attended, chosen[:, : 4 * HS])
    uneven = nt(attended, chosen[:, 4 * HS :])
    share = even[:4] + uneven[4:]
    c_in[col] = jnp.concatenate(
        [
            share[:, :HS],
            share[:, HS : 2 * HS],
            jnp.concatenate([share[:, 2 * HS :], jnp.zeros((4, 64), F32)], axis=1),
            jnp.zeros((4, HS), F32),
        ],
        axis=0,
    ).astype(BF16)
    for peer in (c_peers[2], c_peers[1], c_peers[0]):
        send(c_in.at[col], c_in.at[col], c_send, c_recv, peer)
    arrive(c_in.at[0:3], c_recv)
    final = c_in[0].astype(F32) + c_in[1].astype(F32) + c_in[2].astype(F32) + c_in[3].astype(F32)
    out_ref[0] = jnp.concatenate([final[0:4], final[4:8], final[8:12, :64]], axis=1).astype(BF16)
    arrive(y_in.at[0:3], y_send)
    arrive(z_in.at[0:3], z_send)
    arrive(c_in.at[0:3], c_send)
    arrive(slabs.at[0:7], w_send)


def writer(*refs):
    sems = refs[-1]
    copies = [pltpu.make_async_copy(refs[i], refs[4 + i], sems.at[i]) for i in range(4)]
    for copy in copies:
        copy.start()
    for copy in copies:
        copy.wait()


def per_device(master, grad, first, second, resident, tags, queries, keys, values, lengths):
    flip = functools.partial(jnp.swapaxes, axis1=1, axis2=2)
    dma = pltpu.SemaphoreType.DMA
    rows, width = queries.shape[1], master.shape[2]
    shapes = [(1, width, HS)] * 3 + [(1, rows, width)]
    operands = (
        flip(master), flip(grad), flip(first), flip(second), flip(resident), tags, queries, keys, values, lengths
    )
    held = pl.pallas_call(
        kernel,
        out_shape=[pltpu.VMEM(shape, BF16) for shape in shapes],
        in_specs=[pl.BlockSpec(memory_space=pltpu.HBM)] * 10,
        out_specs=[pl.BlockSpec(memory_space=pltpu.VMEM)] * 4,
        scratch_shapes=[
            pltpu.VMEM((4, 320, 128), BF16),
            pltpu.VMEM((1, 320, 1024), BF16),
            pltpu.SMEM((1,), jnp.int32),
            pltpu.VMEM((1, 4, 1024), BF16),
            pltpu.VMEM((4, 512, 256), BF16),
            pltpu.VMEM((4, 512, 256), BF16),
            pltpu.SMEM((1, 4), jnp.int32),
            pltpu.VMEM((8, 320, 128), BF16),
            pltpu.VMEM((320, 1024), BF16),
            pltpu.VMEM((48, 128), BF16),
            pltpu.VMEM((4, 48, 128), BF16),
            pltpu.VMEM((48, 128), BF16),
            pltpu.VMEM((4, 48, 128), BF16),
            pltpu.VMEM((4, 16, 128), BF16),
            pltpu.SemaphoreType.REGULAR, pltpu.SemaphoreType.REGULAR,
            dma((2,)), dma((4,)), dma, dma, dma, dma,
            dma, dma((3,)), dma, dma, dma, dma, dma, dma, dma,
        ],
        compiler_params=pltpu.CompilerParams(collective_id=0, has_side_effects=True),
    )(
        *[value if value is tags else pltpu.with_memory_space_constraint(value, pltpu.HBM) for value in operands]
    )
    updated, first_new, second_new, projected = pl.pallas_call(
        writer,
        out_shape=[pltpu.HBM(shape, BF16) for shape in shapes],
        in_specs=[pl.BlockSpec(memory_space=pltpu.VMEM)] * 4,
        out_specs=[pl.BlockSpec(memory_space=pltpu.HBM)] * 4,
        scratch_shapes=[dma((4,))],
    )(*[pltpu.with_memory_space_constraint(value, pltpu.VMEM) for value in held])
    return flip(updated), flip(first_new), flip(second_new), projected


def solution(mesh):
    return jax.shard_map(
        per_device,
        mesh=mesh,
        in_specs=(
            P("col", "group", "shard"),
            P("col", "group", "shard"),
            P("col", "group", "shard"),
            P("col", "group", "shard"),
            P("group", "col", "shard"),
            P("group"),
            P("group", None, "col"),
            P("group", None, "shard", "col"),
            P("group", None, "shard", "col"),
            P("group", None),
        ),
        out_specs=(
            P("col", "group", "shard"),
            P("col", "group", "shard"),
            P("col", "group", "shard"),
            P("group", None, "shard"),
        ),
        check_vma=False,
    )
```

```python
import functools

import jax
import jax.numpy as jnp
from jax import lax
from jax.experimental import pallas as pl
from jax.experimental.pallas import tpu as pltpu
from jax.sharding import PartitionSpec as P

HS = 128
MESH = pl.DeviceIdType.MESH
F32 = jnp.float32
BF16 = jnp.bfloat16

beta_one = 0.9
beta_two = 0.999
learn_rate = 0.01
decay = 0.1
adam_eps = 1e-08
correct_one = 1.0
correct_two = 0.6323045752
neg_big = -1e30


def chosen_row(row):
    return row < 2


def adam(master, grad, first, second):
    g32 = grad.astype(F32)
    first_new = beta_one * first.astype(F32) + (1.0 - beta_one) * g32
    second_new = beta_two * second.astype(F32) + (1.0 - beta_two) * g32 * g32
    w32 = master.astype(F32)
    step_size = (
        learn_rate * (first_new / correct_one) / (jnp.sqrt(second_new / correct_two) + adam_eps)
    )
    updated = w32 - step_size - learn_rate * decay * w32
    return updated.astype(BF16), first_new.astype(BF16), second_new.astype(BF16)


def nt(a, b):
    return lax.dot_general(a, b, (((1,), (1,)), ((), ())), preferred_element_type=F32)


def pack(best, total):
    lane = lax.broadcasted_iota(jnp.int32, (32, HS), 1)
    stats = jnp.where(lane == 0, best, jnp.where(lane == 1, total, 0.0)).T[:2]
    return jnp.concatenate([stats, jnp.zeros((2, HS - 32), F32)], axis=1)


def merge(shares, last=False):
    best = functools.reduce(jnp.maximum, [stats[0:1] for _, stats in shares])
    factors = [jnp.exp(stats[0:1] - best) for _, stats in shares]
    total = sum(stats[1:2] * factor for (_, stats), factor in zip(shares, factors))
    if last:
        factors = [factor / total for factor in factors]
    blank = jnp.zeros((8 - len(shares), HS), F32)
    columns = jnp.concatenate(factors + [blank], axis=0).T[:32]
    acc = sum(rows.astype(F32) * columns[:, i : i + 1] for i, (rows, _) in enumerate(shares))
    return acc, jnp.concatenate([best, total], axis=0)


def kernel(
    master_ref, grad_ref, first_ref, second_ref, resident_ref, tags_ref, queries_ref, keys_ref, values_ref, lengths_ref,
    updated_ref, first_out, second_out, out_ref,
    state, resident, tags, queries, keys, values, lengths,
    slabs, chosen, y_out, y_in, z_out, z_in, d_in, y_top, y_tops, z_top, z_tops, d_tops, attended, c_in,
    z_ready, s_ready, small_sem, key_sem, value_sem, state_sem, resident_sem, tags_sem,
    w_send, x_recv, s_recv, y_send, y_recv, z_send, z_recv, d_send, d_recv, e_recv, c_send, c_recv,
):
    group = lax.axis_index("group")
    shard = lax.axis_index("shard")
    col = lax.axis_index("col")
    x, core = group // 2, group % 2
    z, y = shard // 4, shard % 4

    x_peers = [{"group": (x + d) % 4 * 2 + core} for d in (1, 2, 3)]
    y_peers = [{"shard": z * 4 + (y + d) % 4} for d in (1, 2, 3)]
    z_peers = [{"shard": (z + d) % 4 * 4 + y} for d in (1, 2, 3)]
    c_peers = [{"col": (col + d) % 4} for d in (1, 2, 3)]
    sibling = {"group": x * 2 + 1 - core}

    def load(src, dst, sem):
        copy = pltpu.make_async_copy(src, dst, sem)
        copy.start()
        return copy

    q_load = load(queries_ref, queries, small_sem.at[0])
    l_load = load(lengths_ref, lengths, small_sem.at[1])
    k_loads = [load(keys_ref.at[0, r], keys.at[r], key_sem.at[r]) for r in range(4)]
    barrier = pltpu.get_barrier_semaphore()

    def tell(sem, peer):
        pl.semaphore_signal(sem, inc=1, device_id=peer, device_id_type=MESH)

    for peer in y_peers + x_peers + c_peers:
        tell(barrier, peer)
    def tell_late():
        for j in (3, 2):
            for i in range(4):
                tell(barrier, {"shard": j * 4 + i})
        tell(barrier, {"shard": 4 + y})

    chosen_y = chosen_row(y)
    first = (z == 0) & chosen_y
    late = z > 1
    pl.when(first)(tell_late)
    for j in (3, 2):
        pl.when(jnp.logical_not(first) & (z < j))(functools.partial(tell, barrier, {"shard": j * 4 + y}))
    pl.when(jnp.logical_not(first) & (z < 1))(functools.partial(tell, barrier, {"shard": 4 + y}))
    pl.when(core == 0)(functools.partial(tell, barrier, sibling))

    v_loads = [load(values_ref.at[0, r], values.at[r], value_sem.at[r]) for r in range(4)]

    def send(src, dst, send_sem, recv_sem, peer):
        pltpu.make_async_remote_copy(
            src_ref=src, dst_ref=dst, send_sem=send_sem, recv_sem=recv_sem, device_id=peer, device_id_type=MESH
        ).start()

    def arrive(ref, sem):
        pltpu.make_async_copy(ref, ref, sem).wait()

    q_load.wait()
    q32 = queries[0].astype(F32)
    tall = [jnp.concatenate([q32[:, h * HS : (h + 1) * HS] for h in range(4 * k, 4 * k + 4)], axis=0) for k in (0, 1)]
    blank = jnp.zeros((16, HS), F32)
    wide = jnp.concatenate(
        [jnp.concatenate([tall[0], blank], axis=1), jnp.concatenate([blank, tall[1]], axis=1)], axis=0
    )
    row_q = lax.broadcasted_iota(jnp.int32, (32, 2 * HS), 0) % 4
    row = lax.broadcasted_iota(jnp.int32, (32, 512), 0) % 4
    scores = jnp.zeros((32, 512), F32)
    for r in range(4):
        k_loads[r].wait()
        scores = scores + nt(jnp.where(row_q == r, wide, 0.0).astype(BF16), keys[r])
    for i, src in enumerate((master_ref, grad_ref, first_ref, second_ref)):
        load(src.at[0], state.at[i], state_sem)
    r_load = load(resident_ref, resident, resident_sem)
    t_load = load(tags_ref, tags, tags_sem)

    l_load.wait()
    for copy in v_loads:
        copy.wait()
    position = shard * 512 + lax.broadcasted_iota(jnp.int32, (32, 512), 1)
    limit = jnp.where(
        row == 0, lengths[0, 0], jnp.where(row == 1, lengths[0, 1], jnp.where(row == 2, lengths[0, 2], lengths[0, 3]))
    )
    mask = position < limit
    scores = scores * (1.0 / HS**0.5)
    best = jnp.max(jnp.where(mask, scores, neg_big), axis=1, keepdims=True)
    probs = jnp.where(mask, jnp.exp(scores - best), 0.0)
    total = jnp.sum(probs, axis=1, keepdims=True)
    both = jnp.zeros((32, 2 * HS), F32)
    for r in range(4):
        both = both + jnp.dot(
            jnp.where(row == r, probs, 0.0).astype(BF16), values[r], preferred_element_type=F32
        )
    y_out[...] = jnp.concatenate([both[:16, :HS], both[16:, HS:]], axis=0).astype(BF16)
    y_top[...] = pack(best, total)

    several = sum(jnp.where(chosen_row(i), 1, 0) for i in range(4))
    pl.semaphore_wait(barrier, 9 + z + core + jnp.where(late, several - jnp.where(chosen_y, 1, 0), 0))

    def send_direct():
        def send_one(i, place):
            send(y_out, d_in.at[place], d_send.at[0], d_recv.at[z - 2], {"shard": i})
            send(y_top, d_tops.at[place], d_send.at[1], e_recv.at[z - 2], {"shard": i})

        for i in range(4):
            pl.when(chosen_row(i))(functools.partial(send_one, i, (z - 2) * 4 + y))

    pl.when(late)(send_direct)
    for peer in (y_peers[1], y_peers[0], y_peers[2]):
        send(y_out, y_in.at[y], y_send.at[0], y_recv.at[0], peer)
        send(y_top, y_tops.at[y], y_send.at[1], y_recv.at[1], peer)
    for j in (0, 1, 2):
        pl.when(j < z)(functools.partial(tell, z_ready, {"shard": j * 4 + y}))
    pl.when(core == 1)(functools.partial(tell, s_ready, sibling))
    y_in[y] = y_out[...]
    y_tops[y] = y_top[...]

    arrive(state, state_sem)
    updated, first_new, second_new = adam(state[0], state[1], state[2], state[3])
    slabs[group] = updated
    for d in (1, 3, 2):
        send(slabs.at[group], slabs.at[group], w_send, x_recv.at[d - 1], x_peers[d - 1])
    updated_ref[0] = updated
    first_out[0] = first_new
    second_out[0] = second_new

    arrive(y_in.at[0:3], y_recv.at[0])
    arrive(y_tops.at[0:3], y_recv.at[1])
    rows, top = merge([(y_in[i], y_tops[i]) for i in range(4)])
    z_out[...] = rows.astype(BF16)
    z_top[...] = top
    def send_z(j):
        send(z_out, z_in.at[z], z_send.at[0], z_recv.at[0], {"shard": j * 4 + y})
        send(z_top, z_tops.at[z], z_send.at[1], z_recv.at[1], {"shard": j * 4 + y})

    pl.when((z == 1) | late & jnp.logical_not(chosen_y))(functools.partial(send_z, 0))
    for j in (1, 2):
        pl.when(j < z)(functools.partial(send_z, j))
    z_in[z] = z_out[...]
    z_tops[z] = z_top[...]

    def pass_on():
        pl.when(core == 0)(lambda: pl.semaphore_wait(s_ready, 1))
        send(slabs.at[group], slabs.at[group], w_send, s_recv, sibling)
        for d in (1, 3, 2):
            arrive(slabs.at[0], x_recv.at[d - 1])
            block = (x + 4 - d) % 4 * 2 + core
            send(slabs.at[block], slabs.at[block], w_send, s_recv, sibling)

    def send_later():
        pl.semaphore_wait(z_ready, 3 - z)
        for j in (3, 2, 1):
            pl.when(j > z)(functools.partial(send_z, j))

    pl.when(z < 2)(pass_on)
    pl.when(z < 3)(send_later)
    pl.when(z >= 2)(pass_on)
    r_load.wait()
    t_load.wait()
    odd = jnp.full((320, HS), tags[0], jnp.int32) % 2 == 1
    arrive(slabs.at[0:4], s_recv)
    for h in range(8):
        place = (h % 2 * 4 + h // 2) * HS
        chosen[:, place : place + HS] = jnp.where(odd, slabs[h], resident[0, :, h * HS : (h + 1) * HS])

    def finish(shares):
        acc, _ = merge(shares, last=True)
        attended[...] = jnp.concatenate([acc[8 * j : 8 * j + 8] for j in range(4)], axis=1).astype(BF16)

    def finish_first():
        arrive(z_in.at[0], z_recv.at[0])
        arrive(z_tops.at[0], z_recv.at[1])
        arrive(d_in.at[0:4], d_recv.at[1])
        arrive(d_tops.at[0:4], e_recv.at[1])
        running = merge([(z_in[i], z_tops[i]) for i in (0, 1)] + [(d_in[i], d_tops[i]) for i in (4, 5, 6, 7)])
        arrive(d_in.at[0:4], d_recv.at[0])
        arrive(d_tops.at[0:4], e_recv.at[0])
        finish([running] + [(d_in[i], d_tops[i]) for i in (0, 1, 2, 3)])

    def finish_other():
        arrive(z_in.at[0:3], z_recv.at[0])
        arrive(z_tops.at[0:3], z_recv.at[1])
        finish([(z_in[i], z_tops[i]) for i in range(4)])

    pl.when(first)(finish_first)
    pl.when(jnp.logical_not(first))(finish_other)
    even = nt(attended[...], chosen[:, : 4 * HS])
    uneven = nt(attended[...], chosen[:, 4 * HS :])
    share = even[:4] + uneven[4:]
    c_in[col] = jnp.concatenate(
        [
            share[:, :HS],
            share[:, HS : 2 * HS],
            jnp.concatenate([share[:, 2 * HS :], jnp.zeros((4, 64), F32)], axis=1),
            jnp.zeros((4, HS), F32),
        ],
        axis=0,
    ).astype(BF16)
    for peer in (c_peers[2], c_peers[1], c_peers[0]):
        send(c_in.at[col], c_in.at[col], c_send, c_recv, peer)
    arrive(c_in.at[0:3], c_recv)
    final = c_in[0].astype(F32) + c_in[1].astype(F32) + c_in[2].astype(F32) + c_in[3].astype(F32)
    out_ref[0] = jnp.concatenate([final[0:4], final[4:8], final[8:12, :64]], axis=1).astype(BF16)
    arrive(y_in.at[0:3], y_send.at[0])
    arrive(y_tops.at[0:3], y_send.at[1])
    fewer = late & chosen_y

    def sent(count):
        arrive(z_in.at[0:count], z_send.at[0])
        arrive(z_tops.at[0:count], z_send.at[1])

    def sent_direct():
        arrive(d_in.at[0], d_send.at[0])
        arrive(d_tops.at[0], d_send.at[1])

    pl.when(jnp.logical_not(fewer))(functools.partial(sent, 3))
    pl.when(fewer)(functools.partial(sent, 2))
    for i in range(4):
        pl.when(late & chosen_row(i))(sent_direct)
    arrive(c_in.at[0:3], c_send)
    arrive(slabs.at[0:7], w_send)


def writer(*refs):
    sems = refs[-1]
    copies = [pltpu.make_async_copy(refs[i], refs[4 + i], sems.at[i]) for i in range(4)]
    for copy in copies:
        copy.start()
    for copy in copies:
        copy.wait()


def per_device(master, grad, first, second, resident, tags, queries, keys, values, lengths):
    flip = functools.partial(jnp.swapaxes, axis1=1, axis2=2)
    dma = pltpu.SemaphoreType.DMA
    rows, width = queries.shape[1], master.shape[2]
    shapes = [(1, width, HS)] * 3 + [(1, rows, width)]
    operands = (
        flip(master), flip(grad), flip(first), flip(second), flip(resident), tags, queries, keys, values, lengths
    )
    held = pl.pallas_call(
        kernel,
        out_shape=[pltpu.VMEM(shape, BF16) for shape in shapes],
        in_specs=[pl.BlockSpec(memory_space=pltpu.HBM)] * 10,
        out_specs=[pl.BlockSpec(memory_space=pltpu.VMEM)] * 4,
        scratch_shapes=[
            pltpu.VMEM((4, 320, 128), BF16),
            pltpu.VMEM((1, 320, 1024), BF16),
            pltpu.SMEM((1,), jnp.int32),
            pltpu.VMEM((1, 4, 1024), BF16),
            pltpu.VMEM((4, 512, 256), BF16),
            pltpu.VMEM((4, 512, 256), BF16),
            pltpu.SMEM((1, 4), jnp.int32),
            pltpu.VMEM((8, 320, 128), BF16),
            pltpu.VMEM((320, 1024), BF16),
            pltpu.VMEM((32, 128), BF16),
            pltpu.VMEM((4, 32, 128), BF16),
            pltpu.VMEM((32, 128), BF16),
            pltpu.VMEM((4, 32, 128), BF16),
            pltpu.VMEM((8, 32, 128), BF16),
            pltpu.VMEM((2, 128), F32),
            pltpu.VMEM((4, 2, 128), F32),
            pltpu.VMEM((2, 128), F32),
            pltpu.VMEM((4, 2, 128), F32),
            pltpu.VMEM((8, 2, 128), F32),
            pltpu.VMEM((8, 512), BF16),
            pltpu.VMEM((4, 16, 128), BF16),
            pltpu.SemaphoreType.REGULAR, pltpu.SemaphoreType.REGULAR,
            dma((2,)), dma((4,)), dma((4,)), dma, dma, dma,
            dma, dma((3,)), dma, dma((2,)), dma((2,)), dma((2,)), dma((2,)), dma((2,)), dma((2,)), dma((2,)), dma, dma,
        ],
        compiler_params=pltpu.CompilerParams(collective_id=0, has_side_effects=True),
    )(
        *[value if value is tags else pltpu.with_memory_space_constraint(value, pltpu.HBM) for value in operands]
    )
    updated, first_new, second_new, projected = pl.pallas_call(
        writer,
        out_shape=[pltpu.HBM(shape, BF16) for shape in shapes],
        in_specs=[pl.BlockSpec(memory_space=pltpu.VMEM)] * 4,
        out_specs=[pl.BlockSpec(memory_space=pltpu.HBM)] * 4,
        scratch_shapes=[dma((4,))],
    )(*[pltpu.with_memory_space_constraint(value, pltpu.VMEM) for value in held])
    return flip(updated), flip(first_new), flip(second_new), projected


def solution(mesh):
    return jax.shard_map(
        per_device,
        mesh=mesh,
        in_specs=(
            P("col", "group", "shard"),
            P("col", "group", "shard"),
            P("col", "group", "shard"),
            P("col", "group", "shard"),
            P("group", "col", "shard"),
            P("group"),
            P("group", None, "col"),
            P("group", None, "shard", "col"),
            P("group", None, "shard", "col"),
            P("group", None),
        ),
        out_specs=(
            P("col", "group", "shard"),
            P("col", "group", "shard"),
            P("col", "group", "shard"),
            P("group", None, "shard"),
        ),
        check_vma=False,
    )
```

```python
import functools

import jax
import jax.numpy as jnp
from jax import lax
from jax.experimental import pallas as pl
from jax.experimental.pallas import tpu as pltpu
from jax.sharding import PartitionSpec as P

HS = 128
MESH = pl.DeviceIdType.MESH
F32 = jnp.float32
BF16 = jnp.bfloat16

beta_one = 0.9
beta_two = 0.999
learn_rate = 0.01
decay = 0.1
adam_eps = 1e-08
correct_one = 1.0
correct_two = 0.6323045752
neg_big = -1e30


def adam(master, grad, first, second):
    g32 = grad.astype(F32)
    first_new = beta_one * first.astype(F32) + (1.0 - beta_one) * g32
    second_new = beta_two * second.astype(F32) + (1.0 - beta_two) * g32 * g32
    w32 = master.astype(F32)
    step_size = (
        learn_rate * (first_new / correct_one) / (jnp.sqrt(second_new / correct_two) + adam_eps)
    )
    updated = w32 - step_size - learn_rate * decay * w32
    return updated.astype(BF16), first_new.astype(BF16), second_new.astype(BF16)


def nt(a, b):
    return lax.dot_general(a, b, (((1,), (1,)), ((), ())), preferred_element_type=F32)


def pack(best, total):
    lane = lax.broadcasted_iota(jnp.int32, (32, HS), 1)
    stats = jnp.where(lane == 0, best, jnp.where(lane == 1, total, 0.0)).T[:2]
    return jnp.concatenate([stats, jnp.zeros((2, HS - 32), F32)], axis=1)


def merge(shares, last=False):
    best = functools.reduce(jnp.maximum, [stats[0:1] for _, stats in shares])
    factors = [jnp.exp(stats[0:1] - best) for _, stats in shares]
    total = sum(stats[1:2] * factor for (_, stats), factor in zip(shares, factors))
    if last:
        factors = [factor / total for factor in factors]
    blank = jnp.zeros((8 - len(shares), HS), F32)
    columns = jnp.concatenate(factors + [blank], axis=0).T[:32]
    acc = sum(rows.astype(F32) * columns[:, i : i + 1] for i, (rows, _) in enumerate(shares))
    return acc, jnp.concatenate([best, total], axis=0)


def kernel(
    master_ref, grad_ref, first_ref, second_ref, resident_ref, tags_ref, queries_ref, keys_ref, values_ref, lengths_ref,
    updated_ref, first_out, second_out, out_ref,
    state, resident, tags, queries, keys, values, lengths,
    slabs, chosen, y_out, y_in, z_out, z_in, d_in, y_top, y_tops, z_top, z_tops, d_tops, attended, c_in,
    z_ready, s_ready, c_ready, small_sem, key_sem, value_sem, state_sem, resident_sem, tags_sem,
    w_send, x_recv, s_recv, y_send, y_recv, z_send, z_recv, d_send, d_recv, c_send, c_recv,
):
    group = lax.axis_index("group")
    shard = lax.axis_index("shard")
    col = lax.axis_index("col")
    x, core = group // 2, group % 2
    z, y = shard // 4, shard % 4

    x_peers = [{"group": (x + d) % 4 * 2 + core} for d in (1, 2, 3)]
    y_peers = [{"shard": z * 4 + (y + d) % 4} for d in (1, 2, 3)]
    z_peers = [{"shard": (z + d) % 4 * 4 + y} for d in (1, 2, 3)]
    c_peers = [{"col": (col + d) % 4} for d in (1, 2, 3)]
    sibling = {"group": x * 2 + 1 - core}

    def load(src, dst, sem):
        copy = pltpu.make_async_copy(src, dst, sem)
        copy.start()
        return copy

    q_load = load(queries_ref, queries, small_sem.at[0])
    l_load = load(lengths_ref, lengths, small_sem.at[1])
    k_loads = [load(keys_ref.at[0, r], keys.at[r], key_sem.at[r]) for r in range(4)]
    barrier = pltpu.get_barrier_semaphore()

    def tell(sem, peer):
        pl.semaphore_signal(sem, inc=1, device_id=peer, device_id_type=MESH)

    for peer in y_peers + x_peers:
        tell(barrier, peer)
    first, late = z == 0, z == 2

    def tell_first():
        for i in range(4):
            tell(barrier, {"shard": 8 + i})

    pl.when(first)(tell_first)
    pl.when(z == 1)(functools.partial(tell, barrier, {"shard": 8 + y}))
    for j in (3, 1):
        pl.when(z == 0)(functools.partial(tell, barrier, {"shard": 4 * j + y}))
    pl.when(core == 0)(functools.partial(tell, barrier, sibling))
    before = jnp.where(z == 3, 3 - col, col)
    for d in (1, 2, 3):
        peer = {"col": jnp.where(z == 3, 3 - before - d, before + d)}
        pl.when(before + d < 4)(functools.partial(tell, barrier, peer))

    v_loads = [load(values_ref.at[0, r], values.at[r], value_sem.at[r]) for r in range(4)]

    def send(src, dst, send_sem, recv_sem, peer):
        pltpu.make_async_remote_copy(
            src_ref=src, dst_ref=dst, send_sem=send_sem, recv_sem=recv_sem, device_id=peer, device_id_type=MESH
        ).start()

    def arrive(ref, sem):
        pltpu.make_async_copy(ref, ref, sem).wait()

    q_load.wait()
    q32 = queries[0].astype(F32)
    tall = [jnp.concatenate([q32[:, h * HS : (h + 1) * HS] for h in range(4 * k, 4 * k + 4)], axis=0) for k in (0, 1)]
    blank = jnp.zeros((16, HS), F32)
    wide = jnp.concatenate(
        [jnp.concatenate([tall[0], blank], axis=1), jnp.concatenate([blank, tall[1]], axis=1)], axis=0
    )
    row_q = lax.broadcasted_iota(jnp.int32, (32, 2 * HS), 0) % 4
    row = lax.broadcasted_iota(jnp.int32, (32, 512), 0) % 4
    scores = jnp.zeros((32, 512), F32)
    for r in range(4):
        k_loads[r].wait()
        scores = scores + nt(jnp.where(row_q == r, wide, 0.0).astype(BF16), keys[r])
    for i, src in enumerate((master_ref, grad_ref, first_ref, second_ref)):
        load(src.at[0], state.at[i], state_sem)
    r_load = load(resident_ref, resident, resident_sem)
    t_load = load(tags_ref, tags, tags_sem)

    l_load.wait()
    for copy in v_loads:
        copy.wait()
    position = shard * 512 + lax.broadcasted_iota(jnp.int32, (32, 512), 1)
    limit = jnp.where(
        row == 0, lengths[0, 0], jnp.where(row == 1, lengths[0, 1], jnp.where(row == 2, lengths[0, 2], lengths[0, 3]))
    )
    mask = position < limit
    scores = scores * (1.0 / HS**0.5)
    best = jnp.max(jnp.where(mask, scores, neg_big), axis=1, keepdims=True)
    probs = jnp.where(mask, jnp.exp(scores - best), 0.0)
    total = jnp.sum(probs, axis=1, keepdims=True)
    both = jnp.zeros((32, 2 * HS), F32)
    for r in range(4):
        both = both + jnp.dot(
            jnp.where(row == r, probs, 0.0).astype(BF16), values[r], preferred_element_type=F32
        )
    y_out[...] = jnp.concatenate([both[:16, :HS], both[16:, HS:]], axis=0).astype(BF16)
    y_top[...] = pack(best, total)

    told = jnp.where(late, 5, jnp.where(first, 0, 1))
    pl.semaphore_wait(barrier, 6 + core + told + before)

    def send_direct():
        def send_one(i, place):
            send(y_out, d_in.at[place], d_send.at[0], d_recv.at[0], {"shard": i})
            send(y_top, d_tops.at[place], d_send.at[1], d_recv.at[1], {"shard": i})

        for i in range(4):
            send_one(i, y)

    pl.when(late)(send_direct)
    for peer in ({"shard": z * 4 + i} for i in (y + 1 - y % 2 * 2, (y + 2) % 4, 3 - y)):
        send(y_out, y_in.at[y], y_send.at[0], y_recv.at[0], peer)
        send(y_top, y_tops.at[y], y_send.at[1], y_recv.at[1], peer)
    for j in (1, 2, 3):
        pl.when(z == j)(functools.partial(tell, z_ready.at[j], {"shard": y}))
    pl.when(late)(functools.partial(tell, z_ready.at[2], {"shard": 4 + y}))
    pl.when(core == 1)(functools.partial(tell, s_ready, sibling))
    for d in (1, 2, 3):
        peer = {"col": jnp.where(z == 3, 3 - before + d, before - d)}
        pl.when(before >= d)(functools.partial(tell, c_ready, peer))
    y_in[y] = y_out[...]
    y_tops[y] = y_top[...]

    arrive(state, state_sem)
    updated, first_new, second_new = adam(state[0], state[1], state[2], state[3])
    slabs[group] = updated
    for d in (1, 3, 2):
        send(slabs.at[group], slabs.at[group], w_send, x_recv.at[d - 1], x_peers[d - 1])
    updated_ref[0] = updated
    first_out[0] = first_new
    second_out[0] = second_new

    arrive(y_in.at[0:3], y_recv.at[0])
    arrive(y_tops.at[0:3], y_recv.at[1])
    rows, top = merge([(y_in[i], y_tops[i]) for i in range(4)])
    z_out[...] = rows.astype(BF16)
    z_top[...] = top
    def send_z(j):
        send(z_out, z_in.at[z], z_send.at[0], z_recv.at[0], {"shard": j * 4 + y})
        send(z_top, z_tops.at[z], z_send.at[1], z_recv.at[1], {"shard": j * 4 + y})

    def heard(j):
        pl.semaphore_wait(z_ready.at[j], 1)

    pl.when((z == 1) | (z == 3))(functools.partial(send_z, 0))
    pl.when(late)(functools.partial(send_z, 1))

    def block_three():
        heard(1)
        send_z(1)

    pl.when(z == 3)(block_three)
    z_in[z] = z_out[...]
    z_tops[z] = z_top[...]

    def pass_on():
        pl.when(core == 0)(lambda: pl.semaphore_wait(s_ready, 1))
        send(slabs.at[group], slabs.at[group], w_send, s_recv, sibling)
        for d in (1, 3, 2):
            arrive(slabs.at[0], x_recv.at[d - 1])
            block = (x + 4 - d) % 4 * 2 + core
            send(slabs.at[block], slabs.at[block], w_send, s_recv, sibling)

    def block_zero():
        heard(1)
        send_z(1)
        heard(3)
        tell(z_ready.at[1], {"shard": 12 + y})
        tell(z_ready.at[3], {"shard": 4 + y})
        send_z(3)
        heard(2)
        tell(z_ready.at[2], {"shard": 12 + y})
        tell(z_ready.at[3], {"shard": 8 + y})
        send_z(2)

    def block_one():
        heard(2)
        send_z(2)
        heard(3)
        send_z(3)

    def block_two():
        heard(3)
        send_z(3)

    def block_three_late():
        heard(2)
        send_z(2)

    pass_on()
    for j, step in enumerate((block_zero, block_one, block_two, block_three_late)):
        pl.when(z == j)(step)
    r_load.wait()
    t_load.wait()
    odd = jnp.full((320, HS), tags[0], jnp.int32) % 2 == 1
    arrive(slabs.at[0:4], s_recv)
    for h in range(8):
        place = (h % 2 * 4 + h // 2) * HS
        chosen[:, place : place + HS] = jnp.where(odd, slabs[h], resident[0, :, h * HS : (h + 1) * HS])

    def finish(shares):
        acc, _ = merge(shares, last=True)
        attended[...] = jnp.concatenate([acc[8 * j : 8 * j + 8] for j in range(4)], axis=1).astype(BF16)

    def finish_first():
        arrive(z_in.at[0:2], z_recv.at[0])
        arrive(z_tops.at[0:2], z_recv.at[1])
        running = merge([(z_in[i], z_tops[i]) for i in (0, 1, 3)])
        arrive(d_in, d_recv.at[0])
        arrive(d_tops, d_recv.at[1])
        finish([running] + [(d_in[i], d_tops[i]) for i in range(4)])

    def finish_other():
        arrive(z_in.at[0:3], z_recv.at[0])
        arrive(z_tops.at[0:3], z_recv.at[1])
        finish([(z_in[i], z_tops[i]) for i in range(4)])

    pl.when(before < 3)(lambda: pl.semaphore_wait(c_ready, 3 - before))
    pl.when(first)(finish_first)
    pl.when(jnp.logical_not(first))(finish_other)
    even = nt(attended[...], chosen[:, : 4 * HS])
    uneven = nt(attended[...], chosen[:, 4 * HS :])
    share = even[:4] + uneven[4:]
    c_in[col] = jnp.concatenate(
        [
            share[:, :HS],
            share[:, HS : 2 * HS],
            jnp.concatenate([share[:, 2 * HS :], jnp.zeros((4, 64), F32)], axis=1),
            jnp.zeros((4, HS), F32),
        ],
        axis=0,
    ).astype(BF16)
    for peer in (c_peers[2], c_peers[1], c_peers[0]):
        send(c_in.at[col], c_in.at[col], c_send, c_recv, peer)
    arrive(c_in.at[0:3], c_recv)
    final = c_in[0].astype(F32) + c_in[1].astype(F32) + c_in[2].astype(F32) + c_in[3].astype(F32)
    out_ref[0] = jnp.concatenate([final[0:4], final[4:8], final[8:12, :64]], axis=1).astype(BF16)
    arrive(y_in.at[0:3], y_send.at[0])
    arrive(y_tops.at[0:3], y_send.at[1])

    def sent(count):
        arrive(z_in.at[0:count], z_send.at[0])
        arrive(z_tops.at[0:count], z_send.at[1])

    def sent_direct():
        arrive(d_in, d_send.at[0])
        arrive(d_tops, d_send.at[1])

    pl.when(z != 2)(functools.partial(sent, 3))
    pl.when(late)(functools.partial(sent, 2))
    pl.when(late)(sent_direct)
    arrive(c_in.at[0:3], c_send)
    arrive(slabs.at[0:7], w_send)


def writer(*refs):
    sems = refs[-1]
    copies = [pltpu.make_async_copy(refs[i], refs[4 + i], sems.at[i]) for i in range(4)]
    for copy in copies:
        copy.start()
    for copy in copies:
        copy.wait()


def per_device(master, grad, first, second, resident, tags, queries, keys, values, lengths):
    flip = functools.partial(jnp.swapaxes, axis1=1, axis2=2)
    dma = pltpu.SemaphoreType.DMA
    rows, width = queries.shape[1], master.shape[2]
    shapes = [(1, width, HS)] * 3 + [(1, rows, width)]
    operands = (
        flip(master), flip(grad), flip(first), flip(second), flip(resident), tags, queries, keys, values, lengths
    )
    held = pl.pallas_call(
        kernel,
        out_shape=[pltpu.VMEM(shape, BF16) for shape in shapes],
        in_specs=[pl.BlockSpec(memory_space=pltpu.HBM)] * 10,
        out_specs=[pl.BlockSpec(memory_space=pltpu.VMEM)] * 4,
        scratch_shapes=[
            pltpu.VMEM((4, 320, 128), BF16),
            pltpu.VMEM((1, 320, 1024), BF16),
            pltpu.SMEM((1,), jnp.int32),
            pltpu.VMEM((1, 4, 1024), BF16),
            pltpu.VMEM((4, 512, 256), BF16),
            pltpu.VMEM((4, 512, 256), BF16),
            pltpu.SMEM((1, 4), jnp.int32),
            pltpu.VMEM((8, 320, 128), BF16),
            pltpu.VMEM((320, 1024), BF16),
            pltpu.VMEM((32, 128), BF16),
            pltpu.VMEM((4, 32, 128), BF16),
            pltpu.VMEM((32, 128), BF16),
            pltpu.VMEM((4, 32, 128), BF16),
            pltpu.VMEM((4, 32, 128), BF16),
            pltpu.VMEM((2, 128), F32),
            pltpu.VMEM((4, 2, 128), F32),
            pltpu.VMEM((2, 128), F32),
            pltpu.VMEM((4, 2, 128), F32),
            pltpu.VMEM((4, 2, 128), F32),
            pltpu.VMEM((8, 512), BF16),
            pltpu.VMEM((4, 16, 128), BF16),
            pltpu.SemaphoreType.REGULAR((4,)), pltpu.SemaphoreType.REGULAR, pltpu.SemaphoreType.REGULAR,
            dma((2,)), dma((4,)), dma((4,)), dma, dma, dma,
            dma, dma((3,)), dma, dma((2,)), dma((2,)), dma((2,)), dma((2,)), dma((2,)), dma((2,)), dma, dma,
        ],
        compiler_params=pltpu.CompilerParams(collective_id=0, has_side_effects=True),
    )(
        *[value if value is tags else pltpu.with_memory_space_constraint(value, pltpu.HBM) for value in operands]
    )
    updated, first_new, second_new, projected = pl.pallas_call(
        writer,
        out_shape=[pltpu.HBM(shape, BF16) for shape in shapes],
        in_specs=[pl.BlockSpec(memory_space=pltpu.VMEM)] * 4,
        out_specs=[pl.BlockSpec(memory_space=pltpu.HBM)] * 4,
        scratch_shapes=[dma((4,))],
    )(*[pltpu.with_memory_space_constraint(value, pltpu.VMEM) for value in held])
    return flip(updated), flip(first_new), flip(second_new), projected


def solution(mesh):
    return jax.shard_map(
        per_device,
        mesh=mesh,
        in_specs=(
            P("col", "group", "shard"),
            P("col", "group", "shard"),
            P("col", "group", "shard"),
            P("col", "group", "shard"),
            P("group", "col", "shard"),
            P("group"),
            P("group", None, "col"),
            P("group", None, "shard", "col"),
            P("group", None, "shard", "col"),
            P("group", None),
        ),
        out_specs=(
            P("col", "group", "shard"),
            P("col", "group", "shard"),
            P("col", "group", "shard"),
            P("group", None, "shard"),
        ),
        check_vma=False,
    )
```

```python
import functools

import jax
import jax.numpy as jnp
from jax import lax
from jax.experimental import pallas as pl
from jax.experimental.pallas import tpu as pltpu
from jax.sharding import PartitionSpec as P

HS = 128
MESH = pl.DeviceIdType.MESH
F32 = jnp.float32
BF16 = jnp.bfloat16

beta_one = 0.9
beta_two = 0.999
learn_rate = 0.01
decay = 0.1
adam_eps = 1e-08
correct_one = 1.0
correct_two = 0.6323045752
neg_big = -1e30


def adam(master, grad, first, second):
    g32 = grad.astype(F32)
    first_new = beta_one * first.astype(F32) + (1.0 - beta_one) * g32
    second_new = beta_two * second.astype(F32) + (1.0 - beta_two) * g32 * g32
    w32 = master.astype(F32)
    step_size = (
        learn_rate * (first_new / correct_one) / (jnp.sqrt(second_new / correct_two) + adam_eps)
    )
    updated = w32 - step_size - learn_rate * decay * w32
    return updated.astype(BF16), first_new.astype(BF16), second_new.astype(BF16)


def nt(a, b):
    return lax.dot_general(a, b, (((1,), (1,)), ((), ())), preferred_element_type=F32)


def pack(best, total):
    lane = lax.broadcasted_iota(jnp.int32, (32, HS), 1)
    stats = jnp.where(lane == 0, best, jnp.where(lane == 1, total, 0.0)).T[:2]
    return jnp.concatenate([stats, jnp.zeros((2, HS - 32), F32)], axis=1)


def merge(shares, last=False):
    best = functools.reduce(jnp.maximum, [stats[0:1] for _, stats in shares])
    factors = [jnp.exp(stats[0:1] - best) for _, stats in shares]
    total = sum(stats[1:2] * factor for (_, stats), factor in zip(shares, factors))
    if last:
        factors = [factor / total for factor in factors]
    blank = jnp.zeros((8 - len(shares), HS), F32)
    columns = jnp.concatenate(factors + [blank], axis=0).T[:32]
    acc = sum(rows.astype(F32) * columns[:, i : i + 1] for i, (rows, _) in enumerate(shares))
    return acc, jnp.concatenate([best, total], axis=0)


def kernel(
    master_ref, grad_ref, first_ref, second_ref, resident_ref, tags_ref, queries_ref, keys_ref, values_ref, lengths_ref,
    updated_ref, first_out, second_out, out_ref,
    state, resident, tags, queries, keys, values, lengths,
    slabs, chosen, y_out, y_in, z_out, z_in, d_in, y_top, y_tops, z_top, z_tops, d_tops, attended, c_in,
    z_ready, s_ready, c_ready, small_sem, key_sem, value_sem, state_sem, resident_sem, tags_sem,
    x_recv, s_recv, y_recv, z_recv, d_recv, c_recv,
):
    y_send, z_send, d_send = key_sem.at[0:2], key_sem.at[2:4], value_sem.at[0:2]
    w_send, c_send = value_sem.at[2], value_sem.at[3]
    group = lax.axis_index("group")
    shard = lax.axis_index("shard")
    col = lax.axis_index("col")
    x, core = group // 2, group % 2
    z, y = shard // 4, shard % 4

    x_peers = [{"group": (x + d) % 4 * 2 + core} for d in (1, 2, 3)]
    y_peers = [{"shard": z * 4 + (y + d) % 4} for d in (1, 2, 3)]
    z_peers = [{"shard": (z + d) % 4 * 4 + y} for d in (1, 2, 3)]
    c_peers = [{"col": (col + d) % 4} for d in (1, 2, 3)]
    sibling = {"group": x * 2 + 1 - core}

    def load(src, dst, sem):
        copy = pltpu.make_async_copy(src, dst, sem)
        copy.start()
        return copy

    q_load = load(queries_ref, queries, small_sem.at[0])
    l_load = load(lengths_ref, lengths, small_sem.at[1])
    k_loads = [load(keys_ref.at[0, r], keys.at[r], key_sem.at[r]) for r in range(4)]
    barrier = pltpu.get_barrier_semaphore()

    def tell(sem, peer):
        pl.semaphore_signal(sem, inc=1, device_id=peer, device_id_type=MESH)

    for peer in y_peers + x_peers:
        tell(barrier, peer)
    first, late = z == 0, z == 2

    def tell_first():
        for i in range(4):
            tell(barrier, {"shard": 8 + i})

    pl.when(first)(tell_first)
    pl.when(z == 1)(functools.partial(tell, barrier, {"shard": 8 + y}))
    for j in (3, 1):
        pl.when(z == 0)(functools.partial(tell, barrier, {"shard": 4 * j + y}))
    pl.when(core == 0)(functools.partial(tell, barrier, sibling))
    before = jnp.where(z == 3, 3 - col, col)
    for d in (1, 2, 3):
        peer = {"col": jnp.where(z == 3, 3 - before - d, before + d)}
        pl.when(before + d < 4)(functools.partial(tell, barrier, peer))

    v_loads = [load(values_ref.at[0, r], values.at[r], value_sem.at[r]) for r in range(4)]

    def send(src, dst, send_sem, recv_sem, peer):
        pltpu.make_async_remote_copy(
            src_ref=src, dst_ref=dst, send_sem=send_sem, recv_sem=recv_sem, device_id=peer, device_id_type=MESH
        ).start()

    def arrive(ref, sem):
        pltpu.make_async_copy(ref, ref, sem).wait()

    q_load.wait()
    q32 = queries[0].astype(F32)
    tall = [jnp.concatenate([q32[:, h * HS : (h + 1) * HS] for h in range(4 * k, 4 * k + 4)], axis=0) for k in (0, 1)]
    blank = jnp.zeros((16, HS), F32)
    wide = jnp.concatenate(
        [jnp.concatenate([tall[0], blank], axis=1), jnp.concatenate([blank, tall[1]], axis=1)], axis=0
    )
    row_q = lax.broadcasted_iota(jnp.int32, (32, 2 * HS), 0) % 4
    masked = [jnp.where(row_q == r, wide, 0.0).astype(BF16) for r in range(4)]
    row = lax.broadcasted_iota(jnp.int32, (32, 512), 0) % 4
    position = shard * 512 + lax.broadcasted_iota(jnp.int32, (32, 512), 1)
    l_load.wait()
    limit = jnp.where(
        row == 0, lengths[0, 0], jnp.where(row == 1, lengths[0, 1], jnp.where(row == 2, lengths[0, 2], lengths[0, 3]))
    )
    mask = position < limit
    scores = jnp.zeros((32, 512), F32)
    for r in range(4):
        k_loads[r].wait()
        scores = scores + nt(masked[r], keys[r])
    scores = jnp.where(mask, scores * (1.0 / HS**0.5), neg_big)
    best = jnp.max(scores, axis=1, keepdims=True)
    probs = jnp.exp(scores - best)
    total = jnp.sum(probs, axis=1, keepdims=True)
    weights = [jnp.where(row == r, probs, 0.0).astype(BF16) for r in range(4)]
    y_top[...] = pack(best, total)
    for copy in v_loads:
        copy.wait()
    for i, src in enumerate((master_ref, grad_ref, first_ref, second_ref)):
        load(src.at[0], state.at[i], state_sem)
    r_load = load(resident_ref, resident, resident_sem)
    t_load = load(tags_ref, tags, tags_sem)
    both = jnp.dot(
        jnp.concatenate(weights, axis=1), values[...].reshape(2048, 2 * HS), preferred_element_type=F32
    )
    y_out[...] = jnp.concatenate([both[:16, :HS], both[16:, HS:]], axis=0).astype(BF16)

    told = jnp.where(late, 5, jnp.where(first, 0, 1))
    pl.semaphore_wait(barrier, 6 + core + told + before)

    def send_direct():
        def send_one(i, place):
            send(y_out, d_in.at[place], d_send.at[0], d_recv.at[0], {"shard": i})
            send(y_top, d_tops.at[place], d_send.at[1], d_recv.at[1], {"shard": i})

        for i in range(4):
            send_one(i, y)

    pl.when(late)(send_direct)
    for peer in ({"shard": z * 4 + i} for i in (y + 1 - y % 2 * 2, (y + 2) % 4, 3 - y)):
        send(y_out, y_in.at[y], y_send.at[0], y_recv.at[0], peer)
        send(y_top, y_tops.at[y], y_send.at[1], y_recv.at[1], peer)
    for j in (1, 2, 3):
        pl.when(z == j)(functools.partial(tell, z_ready.at[j], {"shard": y}))
    pl.when(late)(functools.partial(tell, z_ready.at[2], {"shard": 4 + y}))
    pl.when(core == 1)(functools.partial(tell, s_ready, sibling))
    for d in (1, 2, 3):
        peer = {"col": jnp.where(z == 3, 3 - before + d, before - d)}
        pl.when(before >= d)(functools.partial(tell, c_ready, peer))
    y_in[y] = y_out[...]
    y_tops[y] = y_top[...]

    arrive(state, state_sem)
    updated, first_new, second_new = adam(state[0], state[1], state[2], state[3])
    slabs[group] = updated
    for d in (1, 3, 2):
        send(slabs.at[group], slabs.at[group], w_send, x_recv.at[d - 1], x_peers[d - 1])
    updated_ref[0] = updated
    first_out[0] = first_new
    second_out[0] = second_new

    arrive(y_in.at[0:3], y_recv.at[0])
    arrive(y_tops.at[0:3], y_recv.at[1])
    rows, top = merge([(y_in[i], y_tops[i]) for i in range(4)])
    z_out[...] = rows.astype(BF16)
    z_top[...] = top
    def send_z(j):
        send(z_out, z_in.at[z], z_send.at[0], z_recv.at[0], {"shard": j * 4 + y})
        send(z_top, z_tops.at[z], z_send.at[1], z_recv.at[1], {"shard": j * 4 + y})

    def heard(j):
        pl.semaphore_wait(z_ready.at[j], 1)

    pl.when((z == 1) | (z == 3))(functools.partial(send_z, 0))
    pl.when(late)(functools.partial(send_z, 1))

    def block_three():
        heard(1)
        send_z(1)

    pl.when(z == 3)(block_three)
    z_in[z] = z_out[...]
    z_tops[z] = z_top[...]

    def pass_on():
        pl.when(core == 0)(lambda: pl.semaphore_wait(s_ready, 1))
        send(slabs.at[group], slabs.at[group], w_send, s_recv, sibling)
        for d in (1, 3, 2):
            arrive(slabs.at[0], x_recv.at[d - 1])
            block = (x + 4 - d) % 4 * 2 + core
            send(slabs.at[block], slabs.at[block], w_send, s_recv, sibling)

    def block_zero():
        heard(1)
        send_z(1)
        heard(3)
        tell(z_ready.at[1], {"shard": 12 + y})
        tell(z_ready.at[3], {"shard": 4 + y})
        send_z(3)
        heard(2)
        tell(z_ready.at[2], {"shard": 12 + y})
        tell(z_ready.at[3], {"shard": 8 + y})
        send_z(2)

    def block_one():
        heard(2)
        send_z(2)
        heard(3)
        send_z(3)

    def block_two():
        heard(3)
        send_z(3)

    def block_three_late():
        heard(2)
        send_z(2)

    pass_on()
    for j, step in enumerate((block_zero, block_one, block_two, block_three_late)):
        pl.when(z == j)(step)
    r_load.wait()
    t_load.wait()
    odd = jnp.full((320, HS), tags[0], jnp.int32) % 2 == 1
    arrive(slabs.at[0:4], s_recv)
    for h in range(8):
        place = h // 2 * HS
        chosen[h % 2, place : place + HS, :] = jnp.where(odd, slabs[h], resident[0, :, h * HS : (h + 1) * HS]).T

    def finish(shares):
        acc, _ = merge(shares, last=True)
        attended[...] = jnp.concatenate([acc[8 * j : 8 * j + 8] for j in range(4)], axis=1).astype(BF16)

    def finish_first():
        arrive(z_in.at[0:2], z_recv.at[0])
        arrive(z_tops.at[0:2], z_recv.at[1])
        running = merge([(z_in[i], z_tops[i]) for i in (0, 1, 3)])
        arrive(d_in, d_recv.at[0])
        arrive(d_tops, d_recv.at[1])
        finish([running] + [(d_in[i], d_tops[i]) for i in range(4)])

    def finish_other():
        arrive(z_in.at[0:3], z_recv.at[0])
        arrive(z_tops.at[0:3], z_recv.at[1])
        finish([(z_in[i], z_tops[i]) for i in range(4)])

    pl.when(before < 3)(lambda: pl.semaphore_wait(c_ready, 3 - before))
    pl.when(first)(finish_first)
    pl.when(jnp.logical_not(first))(finish_other)
    even = jnp.dot(attended[...], chosen[0], preferred_element_type=F32)
    uneven = jnp.dot(attended[...], chosen[1], preferred_element_type=F32)
    share = even[:4] + uneven[4:]
    c_in[col] = jnp.concatenate(
        [
            share[:, :HS],
            share[:, HS : 2 * HS],
            jnp.concatenate([share[:, 2 * HS :], jnp.zeros((4, 64), F32)], axis=1),
            jnp.zeros((4, HS), F32),
        ],
        axis=0,
    ).astype(BF16)
    for peer in (c_peers[2], c_peers[1], c_peers[0]):
        send(c_in.at[col], c_in.at[col], c_send, c_recv, peer)
    arrive(c_in.at[0:3], c_recv)
    final = c_in[0].astype(F32) + c_in[1].astype(F32) + c_in[2].astype(F32) + c_in[3].astype(F32)
    out_ref[0] = jnp.concatenate([final[0:4], final[4:8], final[8:12, :64]], axis=1).astype(BF16)
    arrive(y_in.at[0:3], y_send.at[0])
    arrive(y_tops.at[0:3], y_send.at[1])

    def sent(count):
        arrive(z_in.at[0:count], z_send.at[0])
        arrive(z_tops.at[0:count], z_send.at[1])

    def sent_direct():
        arrive(d_in, d_send.at[0])
        arrive(d_tops, d_send.at[1])

    pl.when(z != 2)(functools.partial(sent, 3))
    pl.when(late)(functools.partial(sent, 2))
    pl.when(late)(sent_direct)
    arrive(c_in.at[0:3], c_send)
    arrive(slabs.at[0:7], w_send)


def writer(*refs):
    sems = refs[-1]
    copies = [pltpu.make_async_copy(refs[i], refs[4 + i], sems.at[i]) for i in range(4)]
    for copy in copies:
        copy.start()
    for copy in copies:
        copy.wait()


def per_device(master, grad, first, second, resident, tags, queries, keys, values, lengths):
    flip = functools.partial(jnp.swapaxes, axis1=1, axis2=2)
    dma = pltpu.SemaphoreType.DMA
    rows, width = queries.shape[1], master.shape[2]
    shapes = [(1, width, HS)] * 3 + [(1, rows, width)]
    operands = (
        flip(master), flip(grad), flip(first), flip(second), flip(resident), tags, queries, keys, values, lengths
    )
    held = pl.pallas_call(
        kernel,
        out_shape=[pltpu.VMEM(shape, BF16) for shape in shapes],
        in_specs=[pl.BlockSpec(memory_space=pltpu.HBM)] * 10,
        out_specs=[pl.BlockSpec(memory_space=pltpu.VMEM)] * 4,
        scratch_shapes=[
            pltpu.VMEM((4, 320, 128), BF16),
            pltpu.VMEM((1, 320, 1024), BF16),
            pltpu.SMEM((1,), jnp.int32),
            pltpu.VMEM((1, 4, 1024), BF16),
            pltpu.VMEM((4, 512, 256), BF16),
            pltpu.VMEM((4, 512, 256), BF16),
            pltpu.SMEM((1, 4), jnp.int32),
            pltpu.VMEM((8, 320, 128), BF16),
            pltpu.VMEM((2, 512, 320), BF16),
            pltpu.VMEM((32, 128), BF16),
            pltpu.VMEM((4, 32, 128), BF16),
            pltpu.VMEM((32, 128), BF16),
            pltpu.VMEM((4, 32, 128), BF16),
            pltpu.VMEM((4, 32, 128), BF16),
            pltpu.VMEM((2, 128), F32),
            pltpu.VMEM((4, 2, 128), F32),
            pltpu.VMEM((2, 128), F32),
            pltpu.VMEM((4, 2, 128), F32),
            pltpu.VMEM((4, 2, 128), F32),
            pltpu.VMEM((8, 512), BF16),
            pltpu.VMEM((4, 16, 128), BF16),
            pltpu.SemaphoreType.REGULAR((4,)), pltpu.SemaphoreType.REGULAR, pltpu.SemaphoreType.REGULAR,
            dma((2,)), dma((4,)), dma((4,)), dma, dma, dma,
            dma((3,)), dma, dma((2,)), dma((2,)), dma((2,)), dma,
        ],
        compiler_params=pltpu.CompilerParams(collective_id=0, has_side_effects=True),
    )(
        *[value if value is tags else pltpu.with_memory_space_constraint(value, pltpu.HBM) for value in operands]
    )
    updated, first_new, second_new, projected = pl.pallas_call(
        writer,
        out_shape=[pltpu.HBM(shape, BF16) for shape in shapes],
        in_specs=[pl.BlockSpec(memory_space=pltpu.VMEM)] * 4,
        out_specs=[pl.BlockSpec(memory_space=pltpu.HBM)] * 4,
        scratch_shapes=[dma((4,))],
    )(*[pltpu.with_memory_space_constraint(value, pltpu.VMEM) for value in held])
    return flip(updated), flip(first_new), flip(second_new), projected


def solution(mesh):
    return jax.shard_map(
        per_device,
        mesh=mesh,
        in_specs=(
            P("col", "group", "shard"),
            P("col", "group", "shard"),
            P("col", "group", "shard"),
            P("col", "group", "shard"),
            P("group", "col", "shard"),
            P("group"),
            P("group", None, "col"),
            P("group", None, "shard", "col"),
            P("group", None, "shard", "col"),
            P("group", None),
        ),
        out_specs=(
            P("col", "group", "shard"),
            P("col", "group", "shard"),
            P("col", "group", "shard"),
            P("group", None, "shard"),
        ),
        check_vma=False,
    )
```

```python
import functools

import jax
import jax.numpy as jnp
from jax import lax
from jax.experimental import pallas as pl
from jax.experimental.pallas import tpu as pltpu
from jax.sharding import PartitionSpec as P

HS = 128
MESH = pl.DeviceIdType.MESH
F32 = jnp.float32
BF16 = jnp.bfloat16

beta_one = 0.9
beta_two = 0.999
learn_rate = 0.01
decay = 0.1
adam_eps = 1e-08
correct_one = 1.0
correct_two = 0.6323045752
neg_big = -1e30


def adam(master, grad, first, second):
    g32 = grad.astype(F32)
    first_new = beta_one * first.astype(F32) + (1.0 - beta_one) * g32
    second_new = beta_two * second.astype(F32) + (1.0 - beta_two) * g32 * g32
    w32 = master.astype(F32)
    step_size = (
        learn_rate * (first_new / correct_one) / (jnp.sqrt(second_new / correct_two) + adam_eps)
    )
    updated = w32 - step_size - learn_rate * decay * w32
    return updated.astype(BF16), first_new.astype(BF16), second_new.astype(BF16)


def nt(a, b):
    return lax.dot_general(a, b, (((1,), (1,)), ((), ())), preferred_element_type=F32)


def pack(best, total):
    lane = lax.broadcasted_iota(jnp.int32, (32, HS), 1)
    stats = jnp.where(lane == 0, best, jnp.where(lane == 1, total, 0.0)).T[:2]
    return jnp.concatenate([stats, jnp.zeros((2, HS - 32), F32)], axis=1)


def merge(shares, last=False):
    best = functools.reduce(jnp.maximum, [stats[0:1] for _, stats in shares])
    factors = [jnp.exp(stats[0:1] - best) for _, stats in shares]
    total = sum(stats[1:2] * factor for (_, stats), factor in zip(shares, factors))
    if last:
        factors = [factor / total for factor in factors]
    blank = jnp.zeros((8 - len(shares), HS), F32)
    columns = jnp.concatenate(factors + [blank], axis=0).T[:32]
    acc = sum(rows.astype(F32) * columns[:, i : i + 1] for i, (rows, _) in enumerate(shares))
    return acc, jnp.concatenate([best, total], axis=0)


def kernel(
    master_ref, grad_ref, first_ref, second_ref, resident_ref, tags_ref, queries_ref, keys_ref, values_ref, lengths_ref,
    updated_ref, first_out, second_out, out_ref,
    state, resident, tags, queries, keys, values, lengths,
    slabs, chosen, y_out, y_in, z_out, z_in, d_in, y_top, y_tops, z_top, z_tops, d_tops, attended, c_in,
    z_ready, s_ready, c_ready, x_ready, small_sem, key_sem, value_sem, state_sem, resident_sem, tags_sem,
    x_recv, s_recv, y_recv, z_recv, d_recv, c_recv,
):
    y_send, z_send, d_send = key_sem.at[0:2], key_sem.at[2:4], value_sem.at[0:2]
    w_send, c_send = value_sem.at[2], value_sem.at[3]
    group = lax.axis_index("group")
    shard = lax.axis_index("shard")
    col = lax.axis_index("col")
    x, core = group // 2, group % 2
    z, y = shard // 4, shard % 4

    x_peers = [{"group": (x + d) % 4 * 2 + core} for d in (1, 2, 3)]
    y_peers = [{"shard": z * 4 + (y + d) % 4} for d in (1, 2, 3)]
    z_peers = [{"shard": (z + d) % 4 * 4 + y} for d in (1, 2, 3)]
    c_peers = [{"col": (col + d) % 4} for d in (1, 2, 3)]
    sibling = {"group": x * 2 + 1 - core}

    def load(src, dst, sem):
        copy = pltpu.make_async_copy(src, dst, sem)
        copy.start()
        return copy

    q_load = load(queries_ref, queries, small_sem.at[0])
    l_load = load(lengths_ref, lengths, small_sem.at[1])
    k_loads = [load(keys_ref.at[0, r], keys.at[r], key_sem.at[r]) for r in range(4)]
    barrier = pltpu.get_barrier_semaphore()

    def tell(sem, peer):
        pl.semaphore_signal(sem, inc=1, device_id=peer, device_id_type=MESH)

    for peer in y_peers:
        tell(barrier, peer)
    for i in (1, 2, 3):
        pl.when(x != i)(functools.partial(tell, barrier, {"group": 2 * i + core}))
    first, late = z == 0, z == 2

    def tell_first():
        for i in range(4):
            tell(barrier, {"shard": 8 + i})

    pl.when(first)(tell_first)
    pl.when(z == 1)(functools.partial(tell, barrier, {"shard": 8 + y}))
    for j in (3, 1):
        pl.when(z == 0)(functools.partial(tell, barrier, {"shard": 4 * j + y}))
    pl.when(core == 0)(functools.partial(tell, barrier, sibling))
    before = jnp.where(z == 3, 3 - col, col)
    for d in (1, 2, 3):
        peer = {"col": jnp.where(z == 3, 3 - before - d, before + d)}
        pl.when(before + d < 4)(functools.partial(tell, barrier, peer))

    v_loads = [load(values_ref.at[0, r], values.at[r], value_sem.at[r]) for r in range(4)]

    def send(src, dst, send_sem, recv_sem, peer):
        pltpu.make_async_remote_copy(
            src_ref=src, dst_ref=dst, send_sem=send_sem, recv_sem=recv_sem, device_id=peer, device_id_type=MESH
        ).start()

    def arrive(ref, sem):
        pltpu.make_async_copy(ref, ref, sem).wait()

    q_load.wait()
    q32 = queries[0].astype(F32)
    tall = [jnp.concatenate([q32[:, h * HS : (h + 1) * HS] for h in range(4 * k, 4 * k + 4)], axis=0) for k in (0, 1)]
    blank = jnp.zeros((16, HS), F32)
    wide = jnp.concatenate(
        [jnp.concatenate([tall[0], blank], axis=1), jnp.concatenate([blank, tall[1]], axis=1)], axis=0
    )
    row_q = lax.broadcasted_iota(jnp.int32, (32, 2 * HS), 0) % 4
    masked = [jnp.where(row_q == r, wide, 0.0).astype(BF16) for r in range(4)]
    row = lax.broadcasted_iota(jnp.int32, (32, 512), 0) % 4
    position = shard * 512 + lax.broadcasted_iota(jnp.int32, (32, 512), 1)
    l_load.wait()
    limit = jnp.where(
        row == 0, lengths[0, 0], jnp.where(row == 1, lengths[0, 1], jnp.where(row == 2, lengths[0, 2], lengths[0, 3]))
    )
    mask = position < limit
    scores = jnp.zeros((32, 512), F32)
    for r in range(4):
        k_loads[r].wait()
        scores = scores + nt(masked[r], keys[r])
    scores = jnp.where(mask, scores * (1.0 / HS**0.5), neg_big)
    best = jnp.max(scores, axis=1, keepdims=True)
    probs = jnp.exp(scores - best)
    total = jnp.sum(probs, axis=1, keepdims=True)
    weights = [jnp.where(row == r, probs, 0.0).astype(BF16) for r in range(4)]
    y_top[...] = pack(best, total)
    for copy in v_loads:
        copy.wait()
    for i, src in enumerate((master_ref, grad_ref, first_ref, second_ref)):
        load(src.at[0], state.at[i], state_sem)
    r_load = load(resident_ref, resident, resident_sem)
    t_load = load(tags_ref, tags, tags_sem)
    both = jnp.dot(
        jnp.concatenate(weights, axis=1), values[...].reshape(2048, 2 * HS), preferred_element_type=F32
    )
    y_out[...] = jnp.concatenate([both[:16, :HS], both[16:, HS:]], axis=0).astype(BF16)

    told = jnp.where(late, 5, jnp.where(first, 0, 1))
    pl.semaphore_wait(barrier, 3 + jnp.where(x == 0, 0, 3) + core + told + before)

    def send_direct():
        def send_one(i, place):
            send(y_out, d_in.at[place], d_send.at[0], d_recv.at[0], {"shard": i})
            send(y_top, d_tops.at[place], d_send.at[1], d_recv.at[1], {"shard": i})

        for i in range(4):
            send_one(i, y)

    pl.when(late)(send_direct)
    for peer in ({"shard": z * 4 + i} for i in (y + 1 - y % 2 * 2, (y + 2) % 4, 3 - y)):
        send(y_out, y_in.at[y], y_send.at[0], y_recv.at[0], peer)
        send(y_top, y_tops.at[y], y_send.at[1], y_recv.at[1], peer)
    for j in (1, 2, 3):
        pl.when(z == j)(functools.partial(tell, z_ready.at[j], {"shard": y}))
    pl.when(late)(functools.partial(tell, z_ready.at[2], {"shard": 4 + y}))
    pl.when(core == 1)(functools.partial(tell, s_ready, sibling))
    pl.when(x > 0)(functools.partial(tell, x_ready, {"group": core}))
    for d in (1, 2, 3):
        peer = {"col": jnp.where(z == 3, 3 - before + d, before - d)}
        pl.when(before >= d)(functools.partial(tell, c_ready, peer))
    y_in[y] = y_out[...]
    y_tops[y] = y_top[...]

    arrive(state, state_sem)
    updated, first_new, second_new = adam(state[0], state[1], state[2], state[3])
    slabs[group] = updated
    pl.when(x == 0)(lambda: pl.semaphore_wait(x_ready, 3))
    for d in (1, 3, 2):
        send(slabs.at[group], slabs.at[group], w_send, x_recv.at[d - 1], x_peers[d - 1])
    updated_ref[0] = updated
    first_out[0] = first_new
    second_out[0] = second_new

    arrive(y_in.at[0:3], y_recv.at[0])
    arrive(y_tops.at[0:3], y_recv.at[1])
    rows, top = merge([(y_in[i], y_tops[i]) for i in range(4)])
    z_out[...] = rows.astype(BF16)
    z_top[...] = top
    def send_z(j):
        send(z_out, z_in.at[z], z_send.at[0], z_recv.at[0], {"shard": j * 4 + y})
        send(z_top, z_tops.at[z], z_send.at[1], z_recv.at[1], {"shard": j * 4 + y})

    def heard(j):
        pl.semaphore_wait(z_ready.at[j], 1)

    pl.when((z == 1) | (z == 3))(functools.partial(send_z, 0))
    pl.when(late)(functools.partial(send_z, 1))

    def block_three():
        heard(1)
        send_z(1)

    pl.when(z == 3)(block_three)
    z_in[z] = z_out[...]
    z_tops[z] = z_top[...]

    def pass_on():
        pl.when(core == 0)(lambda: pl.semaphore_wait(s_ready, 1))
        send(slabs.at[group], slabs.at[group], w_send, s_recv, sibling)
        for d in (1, 3, 2):
            arrive(slabs.at[0], x_recv.at[d - 1])
            block = (x + 4 - d) % 4 * 2 + core
            send(slabs.at[block], slabs.at[block], w_send, s_recv, sibling)

    def block_zero():
        heard(1)
        send_z(1)
        heard(3)
        tell(z_ready.at[1], {"shard": 12 + y})
        tell(z_ready.at[3], {"shard": 4 + y})
        send_z(3)
        heard(2)
        tell(z_ready.at[2], {"shard": 12 + y})
        tell(z_ready.at[3], {"shard": 8 + y})
        send_z(2)

    def block_one():
        heard(2)
        send_z(2)
        heard(3)
        send_z(3)

    def block_two():
        heard(3)
        send_z(3)

    def block_three_late():
        heard(2)
        send_z(2)

    pass_on()
    for j, step in enumerate((block_zero, block_one, block_two, block_three_late)):
        pl.when(z == j)(step)
    r_load.wait()
    t_load.wait()
    odd = jnp.full((320, HS), tags[0], jnp.int32) % 2 == 1
    arrive(slabs.at[0:4], s_recv)
    for h in range(8):
        place = h // 2 * HS
        chosen[h % 2, place : place + HS, :] = jnp.where(odd, slabs[h], resident[0, :, h * HS : (h + 1) * HS]).T

    def finish(shares):
        acc, _ = merge(shares, last=True)
        attended[...] = jnp.concatenate([acc[8 * j : 8 * j + 8] for j in range(4)], axis=1).astype(BF16)

    def finish_first():
        arrive(z_in.at[0:2], z_recv.at[0])
        arrive(z_tops.at[0:2], z_recv.at[1])
        running = merge([(z_in[i], z_tops[i]) for i in (0, 1, 3)])
        arrive(d_in, d_recv.at[0])
        arrive(d_tops, d_recv.at[1])
        finish([running] + [(d_in[i], d_tops[i]) for i in range(4)])

    def finish_other():
        arrive(z_in.at[0:3], z_recv.at[0])
        arrive(z_tops.at[0:3], z_recv.at[1])
        finish([(z_in[i], z_tops[i]) for i in range(4)])

    pl.when(before < 3)(lambda: pl.semaphore_wait(c_ready, 3 - before))
    pl.when(first)(finish_first)
    pl.when(jnp.logical_not(first))(finish_other)
    even = jnp.dot(attended[...], chosen[0], preferred_element_type=F32)
    uneven = jnp.dot(attended[...], chosen[1], preferred_element_type=F32)
    share = even[:4] + uneven[4:]
    c_in[col] = jnp.concatenate(
        [
            share[:, :HS],
            share[:, HS : 2 * HS],
            jnp.concatenate([share[:, 2 * HS :], jnp.zeros((4, 64), F32)], axis=1),
            jnp.zeros((4, HS), F32),
        ],
        axis=0,
    ).astype(BF16)
    for peer in (c_peers[2], c_peers[1], c_peers[0]):
        send(c_in.at[col], c_in.at[col], c_send, c_recv, peer)
    arrive(c_in.at[0:3], c_recv)
    final = c_in[0].astype(F32) + c_in[1].astype(F32) + c_in[2].astype(F32) + c_in[3].astype(F32)
    out_ref[0] = jnp.concatenate([final[0:4], final[4:8], final[8:12, :64]], axis=1).astype(BF16)
    arrive(y_in.at[0:3], y_send.at[0])
    arrive(y_tops.at[0:3], y_send.at[1])

    def sent(count):
        arrive(z_in.at[0:count], z_send.at[0])
        arrive(z_tops.at[0:count], z_send.at[1])

    def sent_direct():
        arrive(d_in, d_send.at[0])
        arrive(d_tops, d_send.at[1])

    pl.when(z != 2)(functools.partial(sent, 3))
    pl.when(late)(functools.partial(sent, 2))
    pl.when(late)(sent_direct)
    arrive(c_in.at[0:3], c_send)
    arrive(slabs.at[0:7], w_send)


def writer(*refs):
    sems = refs[-1]
    copies = [pltpu.make_async_copy(refs[i], refs[4 + i], sems.at[i]) for i in range(4)]
    for copy in copies:
        copy.start()
    for copy in copies:
        copy.wait()


def per_device(master, grad, first, second, resident, tags, queries, keys, values, lengths):
    flip = functools.partial(jnp.swapaxes, axis1=1, axis2=2)
    dma = pltpu.SemaphoreType.DMA
    rows, width = queries.shape[1], master.shape[2]
    shapes = [(1, width, HS)] * 3 + [(1, rows, width)]
    operands = (
        flip(master), flip(grad), flip(first), flip(second), flip(resident), tags, queries, keys, values, lengths
    )
    held = pl.pallas_call(
        kernel,
        out_shape=[pltpu.VMEM(shape, BF16) for shape in shapes],
        in_specs=[pl.BlockSpec(memory_space=pltpu.HBM)] * 10,
        out_specs=[pl.BlockSpec(memory_space=pltpu.VMEM)] * 4,
        scratch_shapes=[
            pltpu.VMEM((4, 320, 128), BF16),
            pltpu.VMEM((1, 320, 1024), BF16),
            pltpu.SMEM((1,), jnp.int32),
            pltpu.VMEM((1, 4, 1024), BF16),
            pltpu.VMEM((4, 512, 256), BF16),
            pltpu.VMEM((4, 512, 256), BF16),
            pltpu.SMEM((1, 4), jnp.int32),
            pltpu.VMEM((8, 320, 128), BF16),
            pltpu.VMEM((2, 512, 320), BF16),
            pltpu.VMEM((32, 128), BF16),
            pltpu.VMEM((4, 32, 128), BF16),
            pltpu.VMEM((32, 128), BF16),
            pltpu.VMEM((4, 32, 128), BF16),
            pltpu.VMEM((4, 32, 128), BF16),
            pltpu.VMEM((2, 128), F32),
            pltpu.VMEM((4, 2, 128), F32),
            pltpu.VMEM((2, 128), F32),
            pltpu.VMEM((4, 2, 128), F32),
            pltpu.VMEM((4, 2, 128), F32),
            pltpu.VMEM((8, 512), BF16),
            pltpu.VMEM((4, 16, 128), BF16),
            pltpu.SemaphoreType.REGULAR((4,)), pltpu.SemaphoreType.REGULAR, pltpu.SemaphoreType.REGULAR,
            pltpu.SemaphoreType.REGULAR,
            dma((2,)), dma((4,)), dma((4,)), dma, dma, dma,
            dma((3,)), dma, dma((2,)), dma((2,)), dma((2,)), dma,
        ],
        compiler_params=pltpu.CompilerParams(collective_id=0, has_side_effects=True),
    )(
        *[value if value is tags else pltpu.with_memory_space_constraint(value, pltpu.HBM) for value in operands]
    )
    updated, first_new, second_new, projected = pl.pallas_call(
        writer,
        out_shape=[pltpu.HBM(shape, BF16) for shape in shapes],
        in_specs=[pl.BlockSpec(memory_space=pltpu.VMEM)] * 4,
        out_specs=[pl.BlockSpec(memory_space=pltpu.HBM)] * 4,
        scratch_shapes=[dma((4,))],
    )(*[pltpu.with_memory_space_constraint(value, pltpu.VMEM) for value in held])
    return flip(updated), flip(first_new), flip(second_new), projected


def solution(mesh):
    return jax.shard_map(
        per_device,
        mesh=mesh,
        in_specs=(
            P("col", "group", "shard"),
            P("col", "group", "shard"),
            P("col", "group", "shard"),
            P("col", "group", "shard"),
            P("group", "col", "shard"),
            P("group"),
            P("group", None, "col"),
            P("group", None, "shard", "col"),
            P("group", None, "shard", "col"),
            P("group", None),
        ),
        out_specs=(
            P("col", "group", "shard"),
            P("col", "group", "shard"),
            P("col", "group", "shard"),
            P("group", None, "shard"),
        ),
        check_vma=False,
    )
```

```python
import functools

import jax
import jax.numpy as jnp
from jax import lax
from jax.experimental import pallas as pl
from jax.experimental.pallas import tpu as pltpu
from jax.sharding import PartitionSpec as P

HS = 128
MESH = pl.DeviceIdType.MESH
F32 = jnp.float32
BF16 = jnp.bfloat16

beta_one = 0.9
beta_two = 0.999
learn_rate = 0.01
decay = 0.1
adam_eps = 1e-08
correct_one = 1.0
correct_two = 0.6323045752
neg_big = -1e30


def adam(master, grad, first, second):
    g32 = grad.astype(F32)
    first_new = beta_one * first.astype(F32) + (1.0 - beta_one) * g32
    second_new = beta_two * second.astype(F32) + (1.0 - beta_two) * g32 * g32
    w32 = master.astype(F32)
    step_size = (
        learn_rate * (first_new / correct_one) / (jnp.sqrt(second_new / correct_two) + adam_eps)
    )
    updated = w32 - step_size - learn_rate * decay * w32
    return updated.astype(BF16), first_new.astype(BF16), second_new.astype(BF16)


def nt(a, b):
    return lax.dot_general(a, b, (((1,), (1,)), ((), ())), preferred_element_type=F32)


def pack(best, total):
    lane = lax.broadcasted_iota(jnp.int32, (32, HS), 1)
    stats = jnp.where(lane == 0, best, jnp.where(lane == 1, total, 0.0)).T[:2]
    return jnp.concatenate([stats, jnp.zeros((2, HS - 32), F32)], axis=1)


def merge(shares, last=False):
    best = functools.reduce(jnp.maximum, [stats[0:1] for _, stats in shares])
    factors = [jnp.exp(stats[0:1] - best) for _, stats in shares]
    total = sum(stats[1:2] * factor for (_, stats), factor in zip(shares, factors))
    if last:
        factors = [factor / total for factor in factors]
    blank = jnp.zeros((8 - len(shares), HS), F32)
    columns = jnp.concatenate(factors + [blank], axis=0).T[:32]
    acc = sum(rows.astype(F32) * columns[:, i : i + 1] for i, (rows, _) in enumerate(shares))
    return acc, jnp.concatenate([best, total], axis=0)


def kernel(
    master_ref, grad_ref, first_ref, second_ref, resident_ref, tags_ref, queries_ref, keys_ref, values_ref, lengths_ref,
    updated_ref, first_out, second_out, out_ref,
    state, resident, tags, queries, keys, values, lengths,
    slabs, chosen, y_out, y_in, z_out, z_in, d_in, y_top, y_tops, z_top, z_tops, d_tops, attended, c_in,
    z_ready, s_ready, c_ready, x_ready, small_sem, key_sem, value_sem, state_sem, resident_sem, tags_sem,
    x_recv, s_recv, y_recv, z_recv, d_recv, c_recv,
):
    y_send, z_send, d_send = key_sem.at[0:2], key_sem.at[2:4], small_sem
    w_send, c_send = state_sem, value_sem
    group = lax.axis_index("group")
    shard = lax.axis_index("shard")
    col = lax.axis_index("col")
    x, core = group // 2, group % 2
    z, y = shard // 4, shard % 4

    x_peers = [{"group": (x + d) % 4 * 2 + core} for d in (1, 2, 3)]
    y_peers = [{"shard": z * 4 + (y + d) % 4} for d in (1, 2, 3)]
    z_peers = [{"shard": (z + d) % 4 * 4 + y} for d in (1, 2, 3)]
    c_peers = [{"col": (col + d) % 4} for d in (1, 2, 3)]
    sibling = {"group": x * 2 + 1 - core}

    def load(src, dst, sem):
        copy = pltpu.make_async_copy(src, dst, sem)
        copy.start()
        return copy

    q_load = load(queries_ref, queries, small_sem.at[0])
    l_load = load(lengths_ref, lengths, small_sem.at[1])
    k_loads = [load(keys_ref.at[0, r], keys.at[r], key_sem.at[r]) for r in range(4)]
    barrier = pltpu.get_barrier_semaphore()

    def tell(sem, peer):
        pl.semaphore_signal(sem, inc=1, device_id=peer, device_id_type=MESH)

    for peer in y_peers:
        tell(barrier, peer)
    for i in (1, 2, 3):
        pl.when(x != i)(functools.partial(tell, barrier, {"group": 2 * i + core}))
    first, late = z == 0, z == 2

    def tell_first():
        for i in range(4):
            tell(barrier, {"shard": 8 + i})

    pl.when(first)(tell_first)
    pl.when(z == 1)(functools.partial(tell, barrier, {"shard": 8 + y}))
    for j in (3, 1):
        pl.when(z == 0)(functools.partial(tell, barrier, {"shard": 4 * j + y}))
    pl.when(core == 0)(functools.partial(tell, barrier, sibling))
    before = jnp.where(z == 3, 3 - col, col)
    for d in (1, 2, 3):
        peer = {"col": jnp.where(z == 3, 3 - before - d, before + d)}
        pl.when(before + d < 4)(functools.partial(tell, barrier, peer))

    v_load = load(values_ref.at[0], values, value_sem)

    def send(src, dst, send_sem, recv_sem, peer):
        pltpu.make_async_remote_copy(
            src_ref=src, dst_ref=dst, send_sem=send_sem, recv_sem=recv_sem, device_id=peer, device_id_type=MESH
        ).start()

    def arrive(ref, sem):
        pltpu.make_async_copy(ref, ref, sem).wait()

    q_load.wait()
    q32 = queries[0].astype(F32)
    tall = [jnp.concatenate([q32[:, h * HS : (h + 1) * HS] for h in range(4 * k, 4 * k + 4)], axis=0) for k in (0, 1)]
    blank = jnp.zeros((16, HS), F32)
    wide = jnp.concatenate(
        [jnp.concatenate([tall[0], blank], axis=1), jnp.concatenate([blank, tall[1]], axis=1)], axis=0
    )
    row_q = lax.broadcasted_iota(jnp.int32, (32, 2 * HS), 0) % 4
    masked = [jnp.where(row_q == r, wide, 0.0).astype(BF16) for r in range(4)]
    row = lax.broadcasted_iota(jnp.int32, (32, 512), 0) % 4
    position = shard * 512 + lax.broadcasted_iota(jnp.int32, (32, 512), 1)
    l_load.wait()
    limit = jnp.where(
        row == 0, lengths[0, 0], jnp.where(row == 1, lengths[0, 1], jnp.where(row == 2, lengths[0, 2], lengths[0, 3]))
    )
    mask = position < limit
    scores = jnp.zeros((32, 512), F32)
    for r in range(4):
        k_loads[r].wait()
        scores = scores + nt(masked[r], keys[r])
    scores = jnp.where(mask, scores * (1.0 / HS**0.5), neg_big)
    best = jnp.max(scores, axis=1, keepdims=True)
    probs = jnp.exp(scores - best)
    total = jnp.sum(probs, axis=1, keepdims=True)
    weights = [jnp.where(row == r, probs, 0.0).astype(BF16) for r in range(4)]
    y_top[...] = pack(best, total)
    v_load.wait()
    for i, src in enumerate((master_ref, grad_ref, first_ref, second_ref)):
        load(src.at[0], state.at[i], state_sem)
    r_load = load(resident_ref, resident, resident_sem)
    t_load = load(tags_ref, tags, tags_sem)
    both = jnp.dot(
        jnp.concatenate(weights, axis=1), values[...].reshape(2048, 2 * HS), preferred_element_type=F32
    )
    y_out[...] = jnp.concatenate([both[:16, :HS], both[16:, HS:]], axis=0).astype(BF16)

    told = jnp.where(late, 5, jnp.where(first, 0, 1))
    pl.semaphore_wait(barrier, 3 + jnp.where(x == 0, 0, 3) + core + told + before)

    def send_direct():
        def send_one(i, place):
            send(y_out, d_in.at[place], d_send.at[0], d_recv.at[0], {"shard": i})
            send(y_top, d_tops.at[place], d_send.at[1], d_recv.at[1], {"shard": i})

        for i in range(4):
            send_one(i, y)

    pl.when(late)(send_direct)
    for peer in ({"shard": z * 4 + i} for i in (y + 1 - y % 2 * 2, (y + 2) % 4, 3 - y)):
        send(y_out, y_in.at[y], y_send.at[0], y_recv.at[0], peer)
        send(y_top, y_tops.at[y], y_send.at[1], y_recv.at[1], peer)
    for j in (1, 2, 3):
        pl.when(z == j)(functools.partial(tell, z_ready.at[j], {"shard": y}))
    pl.when(late)(functools.partial(tell, z_ready.at[2], {"shard": 4 + y}))
    pl.when(core == 1)(functools.partial(tell, s_ready, sibling))
    pl.when(x > 0)(functools.partial(tell, x_ready, {"group": core}))
    for d in (1, 2, 3):
        peer = {"col": jnp.where(z == 3, 3 - before + d, before - d)}
        pl.when(before >= d)(functools.partial(tell, c_ready, peer))
    y_in[y] = y_out[...]
    y_tops[y] = y_top[...]

    arrive(state, state_sem)
    updated, first_new, second_new = adam(state[0], state[1], state[2], state[3])
    slabs[group] = updated
    pl.when(x == 0)(lambda: pl.semaphore_wait(x_ready, 3))
    for d in (1, 3, 2):
        send(slabs.at[group], slabs.at[group], w_send, x_recv.at[d - 1], x_peers[d - 1])
    updated_ref[0] = updated
    first_out[0] = first_new
    second_out[0] = second_new

    arrive(y_in.at[0:3], y_recv.at[0])
    arrive(y_tops.at[0:3], y_recv.at[1])
    rows, top = merge([(y_in[i], y_tops[i]) for i in range(4)])
    z_out[...] = rows.astype(BF16)
    z_top[...] = top
    def send_z(j):
        send(z_out, z_in.at[z], z_send.at[0], z_recv.at[0], {"shard": j * 4 + y})
        send(z_top, z_tops.at[z], z_send.at[1], z_recv.at[1], {"shard": j * 4 + y})

    def heard(j):
        pl.semaphore_wait(z_ready.at[j], 1)

    pl.when((z == 1) | (z == 3))(functools.partial(send_z, 0))
    pl.when(late)(functools.partial(send_z, 1))

    def block_three():
        heard(1)
        send_z(1)

    pl.when(z == 3)(block_three)
    z_in[z] = z_out[...]
    z_tops[z] = z_top[...]

    def pass_on():
        pl.when(core == 0)(lambda: pl.semaphore_wait(s_ready, 1))
        send(slabs.at[group], slabs.at[group], w_send, s_recv, sibling)
        for d in (1, 3, 2):
            arrive(slabs.at[0], x_recv.at[d - 1])
            block = (x + 4 - d) % 4 * 2 + core
            send(slabs.at[block], slabs.at[block], w_send, s_recv, sibling)

    def block_zero():
        heard(1)
        send_z(1)
        heard(3)
        tell(z_ready.at[1], {"shard": 12 + y})
        tell(z_ready.at[3], {"shard": 4 + y})
        send_z(3)
        heard(2)
        tell(z_ready.at[2], {"shard": 12 + y})
        tell(z_ready.at[3], {"shard": 8 + y})
        send_z(2)

    def block_one():
        heard(2)
        send_z(2)
        heard(3)
        send_z(3)

    def block_two():
        heard(3)
        send_z(3)

    def block_three_late():
        heard(2)
        send_z(2)

    pass_on()
    for j, step in enumerate((block_zero, block_one, block_two, block_three_late)):
        pl.when(z == j)(step)
    r_load.wait()
    t_load.wait()
    odd = jnp.full((320, HS), tags[0], jnp.int32) % 2 == 1
    arrive(slabs.at[0:4], s_recv)
    for h in range(8):
        place = h // 2 * HS
        chosen[h % 2, place : place + HS, :] = jnp.where(odd, slabs[h], resident[0, :, h * HS : (h + 1) * HS]).T

    def finish(shares):
        acc, _ = merge(shares, last=True)
        attended[...] = jnp.concatenate([acc[8 * j : 8 * j + 8] for j in range(4)], axis=1).astype(BF16)

    def finish_first():
        arrive(z_in.at[0:2], z_recv.at[0])
        arrive(z_tops.at[0:2], z_recv.at[1])
        running = merge([(z_in[i], z_tops[i]) for i in (0, 1, 3)])
        arrive(d_in, d_recv.at[0])
        arrive(d_tops, d_recv.at[1])
        finish([running] + [(d_in[i], d_tops[i]) for i in range(4)])

    def finish_other():
        arrive(z_in.at[0:3], z_recv.at[0])
        arrive(z_tops.at[0:3], z_recv.at[1])
        finish([(z_in[i], z_tops[i]) for i in range(4)])

    pl.when(before < 3)(lambda: pl.semaphore_wait(c_ready, 3 - before))
    pl.when(first)(finish_first)
    pl.when(jnp.logical_not(first))(finish_other)
    even = jnp.dot(attended[...], chosen[0], preferred_element_type=F32)
    uneven = jnp.dot(attended[...], chosen[1], preferred_element_type=F32)
    share = even[:4] + uneven[4:]
    c_in[col] = jnp.concatenate(
        [
            share[:, :HS],
            share[:, HS : 2 * HS],
            jnp.concatenate([share[:, 2 * HS :], jnp.zeros((4, 64), F32)], axis=1),
            jnp.zeros((4, HS), F32),
        ],
        axis=0,
    ).astype(BF16)
    for peer in (c_peers[2], c_peers[1], c_peers[0]):
        send(c_in.at[col], c_in.at[col], c_send, c_recv, peer)
    arrive(c_in.at[0:3], c_recv)
    final = c_in[0].astype(F32) + c_in[1].astype(F32) + c_in[2].astype(F32) + c_in[3].astype(F32)
    out_ref[0] = jnp.concatenate([final[0:4], final[4:8], final[8:12, :64]], axis=1).astype(BF16)
    arrive(y_in.at[0:3], y_send.at[0])
    arrive(y_tops.at[0:3], y_send.at[1])

    def sent(count):
        arrive(z_in.at[0:count], z_send.at[0])
        arrive(z_tops.at[0:count], z_send.at[1])

    def sent_direct():
        arrive(d_in, d_send.at[0])
        arrive(d_tops, d_send.at[1])

    pl.when(z != 2)(functools.partial(sent, 3))
    pl.when(late)(functools.partial(sent, 2))
    pl.when(late)(sent_direct)
    arrive(c_in.at[0:3], c_send)
    arrive(slabs.at[0:7], w_send)


def writer(*refs):
    sems = refs[-1]
    copies = [pltpu.make_async_copy(refs[i], refs[4 + i], sems.at[i]) for i in range(4)]
    for copy in copies:
        copy.start()
    for copy in copies:
        copy.wait()


def per_device(master, grad, first, second, resident, tags, queries, keys, values, lengths):
    flip = functools.partial(jnp.swapaxes, axis1=1, axis2=2)
    dma = pltpu.SemaphoreType.DMA
    rows, width = queries.shape[1], master.shape[2]
    shapes = [(1, width, HS)] * 3 + [(1, rows, width)]
    operands = (
        flip(master), flip(grad), flip(first), flip(second), flip(resident), tags, queries, keys, values, lengths
    )
    held = pl.pallas_call(
        kernel,
        out_shape=[pltpu.VMEM(shape, BF16) for shape in shapes],
        in_specs=[pl.BlockSpec(memory_space=pltpu.HBM)] * 10,
        out_specs=[pl.BlockSpec(memory_space=pltpu.VMEM)] * 4,
        scratch_shapes=[
            pltpu.VMEM((4, 320, 128), BF16),
            pltpu.VMEM((1, 320, 1024), BF16),
            pltpu.SMEM((1,), jnp.int32),
            pltpu.VMEM((1, 4, 1024), BF16),
            pltpu.VMEM((4, 512, 256), BF16),
            pltpu.VMEM((4, 512, 256), BF16),
            pltpu.SMEM((1, 4), jnp.int32),
            pltpu.VMEM((8, 320, 128), BF16),
            pltpu.VMEM((2, 512, 320), BF16),
            pltpu.VMEM((32, 128), BF16),
            pltpu.VMEM((4, 32, 128), BF16),
            pltpu.VMEM((32, 128), BF16),
            pltpu.VMEM((4, 32, 128), BF16),
            pltpu.VMEM((4, 32, 128), BF16),
            pltpu.VMEM((2, 128), F32),
            pltpu.VMEM((4, 2, 128), F32),
            pltpu.VMEM((2, 128), F32),
            pltpu.VMEM((4, 2, 128), F32),
            pltpu.VMEM((4, 2, 128), F32),
            pltpu.VMEM((8, 512), BF16),
            pltpu.VMEM((4, 16, 128), BF16),
            pltpu.SemaphoreType.REGULAR((4,)), pltpu.SemaphoreType.REGULAR, pltpu.SemaphoreType.REGULAR,
            pltpu.SemaphoreType.REGULAR,
            dma((2,)), dma((4,)), dma, dma, dma, dma,
            dma((3,)), dma, dma((2,)), dma((2,)), dma((2,)), dma,
        ],
        compiler_params=pltpu.CompilerParams(collective_id=0, has_side_effects=True),
    )(
        *[value if value is tags else pltpu.with_memory_space_constraint(value, pltpu.HBM) for value in operands]
    )
    updated, first_new, second_new, projected = pl.pallas_call(
        writer,
        out_shape=[pltpu.HBM(shape, BF16) for shape in shapes],
        in_specs=[pl.BlockSpec(memory_space=pltpu.VMEM)] * 4,
        out_specs=[pl.BlockSpec(memory_space=pltpu.HBM)] * 4,
        scratch_shapes=[dma((4,))],
    )(*[pltpu.with_memory_space_constraint(value, pltpu.VMEM) for value in held])
    return flip(updated), flip(first_new), flip(second_new), projected


def solution(mesh):
    return jax.shard_map(
        per_device,
        mesh=mesh,
        in_specs=(
            P("col", "group", "shard"),
            P("col", "group", "shard"),
            P("col", "group", "shard"),
            P("col", "group", "shard"),
            P("group", "col", "shard"),
            P("group"),
            P("group", None, "col"),
            P("group", None, "shard", "col"),
            P("group", None, "shard", "col"),
            P("group", None),
        ),
        out_specs=(
            P("col", "group", "shard"),
            P("col", "group", "shard"),
            P("col", "group", "shard"),
            P("group", None, "shard"),
        ),
        check_vma=False,
    )
```

```python
import functools

import jax
import jax.numpy as jnp
from jax import lax
from jax.experimental import pallas as pl
from jax.experimental.pallas import tpu as pltpu
from jax.sharding import PartitionSpec as P

HS = 128
MESH = pl.DeviceIdType.MESH
F32 = jnp.float32
BF16 = jnp.bfloat16

beta_one = 0.9
beta_two = 0.999
learn_rate = 0.01
decay = 0.1
adam_eps = 1e-08
correct_one = 1.0
correct_two = 0.6323045752
neg_big = -1e30


def adam(master, grad, first, second):
    g32 = grad.astype(F32)
    first_new = beta_one * first.astype(F32) + (1.0 - beta_one) * g32
    second_new = beta_two * second.astype(F32) + (1.0 - beta_two) * g32 * g32
    w32 = master.astype(F32)
    step_size = (
        learn_rate * (first_new / correct_one) / (jnp.sqrt(second_new / correct_two) + adam_eps)
    )
    updated = w32 - step_size - learn_rate * decay * w32
    return updated.astype(BF16), first_new.astype(BF16), second_new.astype(BF16)


def nt(a, b):
    return lax.dot_general(a, b, (((1,), (1,)), ((), ())), preferred_element_type=F32)


def pack(best, total):
    lane = lax.broadcasted_iota(jnp.int32, (32, HS), 1)
    stats = jnp.where(lane == 0, best, jnp.where(lane == 1, total, 0.0)).T[:2]
    return jnp.concatenate([stats, jnp.zeros((2, HS - 32), F32)], axis=1)


def merge(shares, last=False):
    best = functools.reduce(jnp.maximum, [stats[0:1] for _, stats in shares])
    factors = [jnp.exp(stats[0:1] - best) for _, stats in shares]
    total = sum(stats[1:2] * factor for (_, stats), factor in zip(shares, factors))
    if last:
        factors = [factor / total for factor in factors]
    blank = jnp.zeros((8 - len(shares), HS), F32)
    columns = jnp.concatenate(factors + [blank], axis=0).T[:32]
    acc = sum(rows.astype(F32) * columns[:, i : i + 1] for i, (rows, _) in enumerate(shares))
    return acc, jnp.concatenate([best, total], axis=0)


def kernel(
    master_ref, grad_ref, first_ref, second_ref, resident_ref, tags_ref, queries_ref, keys_ref, values_ref, lengths_ref,
    updated_ref, first_out, second_out, out_ref,
    state, resident, tags, queries, keys, values, lengths,
    slabs, chosen, y_out, y_in, z_out, z_in, d_in, y_top, y_tops, z_top, z_tops, d_tops, attended, c_in,
    z_ready, s_ready, c_ready, x_ready, small_sem, key_sem, value_sem, state_sem, resident_sem, tags_sem,
    x_recv, s_recv, y_recv, z_recv, d_recv, c_recv,
):
    y_send, z_send, d_send = key_sem.at[0:2], key_sem.at[2:4], value_sem.at[0:2]
    w_send, c_send = value_sem.at[2], value_sem.at[3]
    group = lax.axis_index("group")
    shard = lax.axis_index("shard")
    col = lax.axis_index("col")
    x, core = group // 2, group % 2
    z, y = shard // 4, shard % 4

    x_peers = [{"group": (x + d) % 4 * 2 + core} for d in (1, 2, 3)]
    y_peers = [{"shard": z * 4 + (y + d) % 4} for d in (1, 2, 3)]
    z_peers = [{"shard": (z + d) % 4 * 4 + y} for d in (1, 2, 3)]
    c_peers = [{"col": (col + d) % 4} for d in (1, 2, 3)]
    sibling = {"group": x * 2 + 1 - core}

    def load(src, dst, sem):
        copy = pltpu.make_async_copy(src, dst, sem)
        copy.start()
        return copy

    q_load = load(queries_ref, queries, small_sem.at[0])
    l_load = load(lengths_ref, lengths, small_sem.at[1])
    k_loads = [load(keys_ref.at[0, r], keys.at[:, 256 * r : 256 * r + 256], key_sem.at[r]) for r in range(4)]
    barrier = pltpu.get_barrier_semaphore()

    def tell(sem, peer):
        pl.semaphore_signal(sem, inc=1, device_id=peer, device_id_type=MESH)

    for peer in y_peers:
        tell(barrier, peer)
    for i in (1, 2, 3):
        pl.when(x != i)(functools.partial(tell, barrier, {"group": 2 * i + core}))
    first, late = z == 0, z == 2

    def tell_first():
        for i in range(4):
            tell(barrier, {"shard": 8 + i})

    pl.when(first)(tell_first)
    pl.when(z == 1)(functools.partial(tell, barrier, {"shard": 8 + y}))
    for j in (3, 1):
        pl.when(z == 0)(functools.partial(tell, barrier, {"shard": 4 * j + y}))
    pl.when(core == 0)(functools.partial(tell, barrier, sibling))
    before = jnp.where(z == 3, 3 - col, col)
    for d in (1, 2, 3):
        peer = {"col": jnp.where(z == 3, 3 - before - d, before + d)}
        pl.when(before + d < 4)(functools.partial(tell, barrier, peer))

    v_loads = [load(values_ref.at[0, r], values.at[r], value_sem.at[r]) for r in range(4)]

    def send(src, dst, send_sem, recv_sem, peer):
        pltpu.make_async_remote_copy(
            src_ref=src, dst_ref=dst, send_sem=send_sem, recv_sem=recv_sem, device_id=peer, device_id_type=MESH
        ).start()

    def arrive(ref, sem):
        pltpu.make_async_copy(ref, ref, sem).wait()

    q_load.wait()
    q32 = queries[0].astype(F32)
    tall = [jnp.concatenate([q32[:, h * HS : (h + 1) * HS] for h in range(4 * k, 4 * k + 4)], axis=0) for k in (0, 1)]
    blank = jnp.zeros((16, HS), F32)
    wide = jnp.concatenate(
        [jnp.concatenate([tall[0], blank], axis=1), jnp.concatenate([blank, tall[1]], axis=1)], axis=0
    )
    row_q = lax.broadcasted_iota(jnp.int32, (32, 2 * HS), 0) % 4
    masked = [jnp.where(row_q == r, wide, 0.0).astype(BF16) for r in range(4)]
    row = lax.broadcasted_iota(jnp.int32, (32, 512), 0) % 4
    position = shard * 512 + lax.broadcasted_iota(jnp.int32, (32, 512), 1)
    l_load.wait()
    limit = jnp.where(
        row == 0, lengths[0, 0], jnp.where(row == 1, lengths[0, 1], jnp.where(row == 2, lengths[0, 2], lengths[0, 3]))
    )
    mask = position < limit
    for copy in k_loads:
        copy.wait()
    scores = nt(jnp.concatenate(masked, axis=1), keys[...])
    scores = jnp.where(mask, scores * (1.0 / HS**0.5), neg_big)
    best = jnp.max(scores, axis=1, keepdims=True)
    probs = jnp.exp(scores - best)
    total = jnp.sum(probs, axis=1, keepdims=True)
    weights = [jnp.where(row == r, probs, 0.0).astype(BF16) for r in range(4)]
    y_top[...] = pack(best, total)
    for copy in v_loads:
        copy.wait()
    for i, src in enumerate((master_ref, grad_ref, first_ref, second_ref)):
        load(src.at[0], state.at[i], state_sem)
    r_load = load(resident_ref, resident, resident_sem)
    t_load = load(tags_ref, tags, tags_sem)
    both = jnp.dot(
        jnp.concatenate(weights, axis=1), values[...].reshape(2048, 2 * HS), preferred_element_type=F32
    )
    y_out[...] = jnp.concatenate([both[:16, :HS], both[16:, HS:]], axis=0).astype(BF16)

    told = jnp.where(late, 5, jnp.where(first, 0, 1))
    pl.semaphore_wait(barrier, 3 + jnp.where(x == 0, 0, 3) + core + told + before)

    def send_direct():
        def send_one(i, place):
            send(y_out, d_in.at[place], d_send.at[0], d_recv.at[0], {"shard": i})
            send(y_top, d_tops.at[place], d_send.at[1], d_recv.at[1], {"shard": i})

        for i in range(4):
            send_one(i, y)

    pl.when(late)(send_direct)
    for peer in ({"shard": z * 4 + i} for i in (y + 1 - y % 2 * 2, (y + 2) % 4, 3 - y)):
        send(y_out, y_in.at[y], y_send.at[0], y_recv.at[0], peer)
        send(y_top, y_tops.at[y], y_send.at[1], y_recv.at[1], peer)
    for j in (1, 2, 3):
        pl.when(z == j)(functools.partial(tell, z_ready.at[j], {"shard": y}))
    pl.when(late)(functools.partial(tell, z_ready.at[2], {"shard": 4 + y}))
    pl.when(core == 1)(functools.partial(tell, s_ready, sibling))
    pl.when(x > 0)(functools.partial(tell, x_ready, {"group": core}))
    for d in (1, 2, 3):
        peer = {"col": jnp.where(z == 3, 3 - before + d, before - d)}
        pl.when(before >= d)(functools.partial(tell, c_ready, peer))
    y_in[y] = y_out[...]
    y_tops[y] = y_top[...]

    arrive(state, state_sem)
    updated, first_new, second_new = adam(state[0], state[1], state[2], state[3])
    slabs[group] = updated
    pl.when(x == 0)(lambda: pl.semaphore_wait(x_ready, 3))
    for d in (1, 3, 2):
        send(slabs.at[group], slabs.at[group], w_send, x_recv.at[d - 1], x_peers[d - 1])
    updated_ref[0] = updated
    first_out[0] = first_new
    second_out[0] = second_new

    arrive(y_in.at[0:3], y_recv.at[0])
    arrive(y_tops.at[0:3], y_recv.at[1])
    rows, top = merge([(y_in[i], y_tops[i]) for i in range(4)])
    z_out[...] = rows.astype(BF16)
    z_top[...] = top
    def send_z(j):
        send(z_out, z_in.at[z], z_send.at[0], z_recv.at[0], {"shard": j * 4 + y})
        send(z_top, z_tops.at[z], z_send.at[1], z_recv.at[1], {"shard": j * 4 + y})

    def heard(j):
        pl.semaphore_wait(z_ready.at[j], 1)

    pl.when((z == 1) | (z == 3))(functools.partial(send_z, 0))
    pl.when(late)(functools.partial(send_z, 1))

    def block_three():
        heard(1)
        send_z(1)

    pl.when(z == 3)(block_three)
    z_in[z] = z_out[...]
    z_tops[z] = z_top[...]

    def pass_on():
        pl.when(core == 0)(lambda: pl.semaphore_wait(s_ready, 1))
        send(slabs.at[group], slabs.at[group], w_send, s_recv, sibling)
        for d in (1, 3, 2):
            arrive(slabs.at[0], x_recv.at[d - 1])
            block = (x + 4 - d) % 4 * 2 + core
            send(slabs.at[block], slabs.at[block], w_send, s_recv, sibling)

    def block_zero():
        heard(1)
        send_z(1)
        heard(3)
        tell(z_ready.at[1], {"shard": 12 + y})
        tell(z_ready.at[3], {"shard": 4 + y})
        send_z(3)
        heard(2)
        tell(z_ready.at[2], {"shard": 12 + y})
        tell(z_ready.at[3], {"shard": 8 + y})
        send_z(2)

    def block_one():
        heard(2)
        send_z(2)
        heard(3)
        send_z(3)

    def block_two():
        heard(3)
        send_z(3)

    def block_three_late():
        heard(2)
        send_z(2)

    pass_on()
    for j, step in enumerate((block_zero, block_one, block_two, block_three_late)):
        pl.when(z == j)(step)
    r_load.wait()
    t_load.wait()
    odd = jnp.full((320, HS), tags[0], jnp.int32) % 2 == 1
    arrive(slabs.at[0:4], s_recv)
    for h in range(8):
        place = h // 2 * HS
        chosen[h % 2, place : place + HS, :] = jnp.where(odd, slabs[h], resident[0, :, h * HS : (h + 1) * HS]).T

    def finish(shares):
        acc, _ = merge(shares, last=True)
        attended[...] = jnp.concatenate([acc[8 * j : 8 * j + 8] for j in range(4)], axis=1).astype(BF16)

    def finish_first():
        arrive(z_in.at[0:2], z_recv.at[0])
        arrive(z_tops.at[0:2], z_recv.at[1])
        running = merge([(z_in[i], z_tops[i]) for i in (0, 1, 3)])
        arrive(d_in, d_recv.at[0])
        arrive(d_tops, d_recv.at[1])
        finish([running] + [(d_in[i], d_tops[i]) for i in range(4)])

    def finish_other():
        arrive(z_in.at[0:3], z_recv.at[0])
        arrive(z_tops.at[0:3], z_recv.at[1])
        finish([(z_in[i], z_tops[i]) for i in range(4)])

    pl.when(before < 3)(lambda: pl.semaphore_wait(c_ready, 3 - before))
    pl.when(first)(finish_first)
    pl.when(jnp.logical_not(first))(finish_other)
    even = jnp.dot(attended[...], chosen[0], preferred_element_type=F32)
    uneven = jnp.dot(attended[...], chosen[1], preferred_element_type=F32)
    share = even[:4] + uneven[4:]
    c_in[col] = jnp.concatenate(
        [
            share[:, :HS],
            share[:, HS : 2 * HS],
            jnp.concatenate([share[:, 2 * HS :], jnp.zeros((4, 64), F32)], axis=1),
            jnp.zeros((4, HS), F32),
        ],
        axis=0,
    ).astype(BF16)
    for peer in (c_peers[2], c_peers[1], c_peers[0]):
        send(c_in.at[col], c_in.at[col], c_send, c_recv, peer)
    arrive(c_in.at[0:3], c_recv)
    final = c_in[0].astype(F32) + c_in[1].astype(F32) + c_in[2].astype(F32) + c_in[3].astype(F32)
    out_ref[0] = jnp.concatenate([final[0:4], final[4:8], final[8:12, :64]], axis=1).astype(BF16)
    arrive(y_in.at[0:3], y_send.at[0])
    arrive(y_tops.at[0:3], y_send.at[1])

    def sent(count):
        arrive(z_in.at[0:count], z_send.at[0])
        arrive(z_tops.at[0:count], z_send.at[1])

    def sent_direct():
        arrive(d_in, d_send.at[0])
        arrive(d_tops, d_send.at[1])

    pl.when(z != 2)(functools.partial(sent, 3))
    pl.when(late)(functools.partial(sent, 2))
    pl.when(late)(sent_direct)
    arrive(c_in.at[0:3], c_send)
    arrive(slabs.at[0:7], w_send)


def writer(*refs):
    sems = refs[-1]
    copies = [pltpu.make_async_copy(refs[i], refs[4 + i], sems.at[i]) for i in range(4)]
    for copy in copies:
        copy.start()
    for copy in copies:
        copy.wait()


def per_device(master, grad, first, second, resident, tags, queries, keys, values, lengths):
    flip = functools.partial(jnp.swapaxes, axis1=1, axis2=2)
    dma = pltpu.SemaphoreType.DMA
    rows, width = queries.shape[1], master.shape[2]
    shapes = [(1, width, HS)] * 3 + [(1, rows, width)]
    operands = (
        flip(master), flip(grad), flip(first), flip(second), flip(resident), tags, queries, keys, values, lengths
    )
    held = pl.pallas_call(
        kernel,
        out_shape=[pltpu.VMEM(shape, BF16) for shape in shapes],
        in_specs=[pl.BlockSpec(memory_space=pltpu.HBM)] * 10,
        out_specs=[pl.BlockSpec(memory_space=pltpu.VMEM)] * 4,
        scratch_shapes=[
            pltpu.VMEM((4, 320, 128), BF16),
            pltpu.VMEM((1, 320, 1024), BF16),
            pltpu.SMEM((1,), jnp.int32),
            pltpu.VMEM((1, 4, 1024), BF16),
            pltpu.VMEM((512, 1024), BF16),
            pltpu.VMEM((4, 512, 256), BF16),
            pltpu.SMEM((1, 4), jnp.int32),
            pltpu.VMEM((8, 320, 128), BF16),
            pltpu.VMEM((2, 512, 320), BF16),
            pltpu.VMEM((32, 128), BF16),
            pltpu.VMEM((4, 32, 128), BF16),
            pltpu.VMEM((32, 128), BF16),
            pltpu.VMEM((4, 32, 128), BF16),
            pltpu.VMEM((4, 32, 128), BF16),
            pltpu.VMEM((2, 128), F32),
            pltpu.VMEM((4, 2, 128), F32),
            pltpu.VMEM((2, 128), F32),
            pltpu.VMEM((4, 2, 128), F32),
            pltpu.VMEM((4, 2, 128), F32),
            pltpu.VMEM((8, 512), BF16),
            pltpu.VMEM((4, 16, 128), BF16),
            pltpu.SemaphoreType.REGULAR((4,)), pltpu.SemaphoreType.REGULAR, pltpu.SemaphoreType.REGULAR,
            pltpu.SemaphoreType.REGULAR,
            dma((2,)), dma((4,)), dma((4,)), dma, dma, dma,
            dma((3,)), dma, dma((2,)), dma((2,)), dma((2,)), dma,
        ],
        compiler_params=pltpu.CompilerParams(collective_id=0, has_side_effects=True),
    )(
        *[value if value is tags else pltpu.with_memory_space_constraint(value, pltpu.HBM) for value in operands]
    )
    updated, first_new, second_new, projected = pl.pallas_call(
        writer,
        out_shape=[pltpu.HBM(shape, BF16) for shape in shapes],
        in_specs=[pl.BlockSpec(memory_space=pltpu.VMEM)] * 4,
        out_specs=[pl.BlockSpec(memory_space=pltpu.HBM)] * 4,
        scratch_shapes=[dma((4,))],
    )(*[pltpu.with_memory_space_constraint(value, pltpu.VMEM) for value in held])
    return flip(updated), flip(first_new), flip(second_new), projected


def solution(mesh):
    return jax.shard_map(
        per_device,
        mesh=mesh,
        in_specs=(
            P("col", "group", "shard"),
            P("col", "group", "shard"),
            P("col", "group", "shard"),
            P("col", "group", "shard"),
            P("group", "col", "shard"),
            P("group"),
            P("group", None, "col"),
            P("group", None, "shard", "col"),
            P("group", None, "shard", "col"),
            P("group", None),
        ),
        out_specs=(
            P("col", "group", "shard"),
            P("col", "group", "shard"),
            P("col", "group", "shard"),
            P("group", None, "shard"),
        ),
        check_vma=False,
    )
```
